128 devices in a mesh: coil: 4 (over z), slab: 32 (over y, x, core).
Axes of the slice: x: 4, y: 4, z: 4, core: 2. Of those that a mesh axis runs over, the one named last changes fastest.
Arguments:
- image: float32 [2, 256, 256, 256], P(None, 'slab'), may hold values from -6 to 6
- sens: float32 [4, 2, 256, 256, 256], P('coil', None, 'slab'), may hold values from -6 to 6
- weights: bfloat16 [8192, 128, 128], P('slab'), may hold values from -0.5 to 0.5
- bins: int32 [8192], P('slab'), may hold values from 0 to 4095
- counts: int32 [32], P('slab'), may hold values from 32 to 256, as said below
Outputs:
- result: float32 [2, 256, 256, 256], P(None, 'slab', 'coil')
The draws below stay inside these ranges and needn't reach their ends.
Inputs may be any that keep to these rules, and one draw needn't show every extreme that they name: The two slabs at the middle of the second dimension hold 256 live tiles; counts fall towards the edges of k-space.
All inputs are finite; a program needn't handle non-finite values.
Results may differ from the reference program's by a relative error of at most 0.0003.
Values sent between devices are 32-bit elements; how exact they have to be, the bound alone decides.
A program may use at most 128 MiB of HBM per device.

```python
import jax
import jax.numpy as jnp
from jax import lax

NX = 256
NY = 256
NZ = 256
COILS = 4
TILE = 128
CAP = 256
SLABS = 32
TILES = 8192
GRID_TILES = 4096


def draw_counts(key, part):
    key = jax.random.fold_in(key, 7)
    slab_ids = jnp.arange(SLABS, dtype=jnp.int32)
    distance = jnp.abs(2 * slab_ids + 1 - SLABS)
    jitter = jax.random.randint(key, (SLABS,), 0, max(CAP // 8, 1))
    value = CAP - 3 * CAP * distance // (4 * SLABS) - jitter
    return jnp.where(distance <= 1, CAP, value).astype(jnp.int32)


def set_ends(result, stream_key, least, top_value):
    extent = result.shape
    spot = [jax.random.randint(jax.random.fold_in(stream_key, axis), (), 0, extent[axis]) for axis in range(len(extent))]
    result = result.at[tuple(spot)].set(least)
    longest = extent.index(max(extent))
    spot[longest] = (spot[longest] + 1) % extent[longest]
    return result.at[tuple(spot)].set(top_value)


def shard_levels(stream_key, dims, cuts, least, high):
    loudness = 1.0
    for dim, blocks in cuts:
        draws = jax.random.uniform(jax.random.fold_in(jax.random.fold_in(stream_key, 6), dim), (blocks,), jnp.float32, least / len(cuts), high / len(cuts))
        loudness = loudness * jnp.repeat(jnp.exp(draws), dims[dim] // blocks).reshape((-1,) + (1,) * (len(dims) - 1 - dim))
    return loudness


def scatter_about(stream_key, dims, spread, most, cuts=(), kind=jnp.bfloat16):
    values = jax.random.normal(stream_key, dims, jnp.float32) * spread
    if len(cuts) > 0:
        values = shard_levels(stream_key, dims, cuts, -0.22, 0.18) * values
    return jnp.clip(values, min=-most, max=most).astype(kind)


def setup_inputs(seed: int = 0) -> dict:
    arg_keys = jax.random.split(jax.random.key(seed), 6)
    return {
        "image": scatter_about(arg_keys[0], (2, NX, NY, NZ), 1.0, 6.0, ((1, 32),), jnp.float32),
        "sens": scatter_about(arg_keys[1], (COILS, 2, NX, NY, NZ), 1.0, 6.0, ((0, 4), (2, 32)), jnp.float32),
        "weights": scatter_about(arg_keys[2], (TILES, TILE, TILE), TILE ** -0.5, 0.5, ((0, 32),)),
        "bins": set_ends(jax.random.randint(arg_keys[3], (TILES,), 0, GRID_TILES), jax.random.fold_in(arg_keys[3], 1), 0, GRID_TILES - 1).astype(jnp.int32),
        "counts": draw_counts(jax.random.fold_in(arg_keys[5], 71), 0),
    }


def grid_slab(args):
    slab_weights, slab_bins, slab_count, tiles = args
    tile_weights = slab_weights.astype(jnp.float32)
    picked = tiles[:, slab_bins]
    samples = jnp.einsum('jsc,rjc->rjs', tile_weights, picked, precision=lax.Precision.HIGHEST)
    back = jnp.einsum('jsc,rjs->rjc', tile_weights, samples, precision=lax.Precision.HIGHEST)
    keep = jnp.arange(CAP, dtype=jnp.int32) < slab_count
    back = jnp.where(keep[None, :, None], back, jnp.zeros_like(back))
    return jnp.zeros_like(tiles).at[:, slab_bins].add(back)


def reference(image, sens, weights, bins, counts):
    height = NY // SLABS
    field = image[0] + 1j * image[1]
    total = jnp.zeros_like(field)
    slab_weights = weights.reshape(SLABS, CAP, TILE, TILE)
    slab_bins = bins.reshape(SLABS, CAP)
    for coil_index in range(COILS):
        coil_map = sens[coil_index, 0] + 1j * sens[coil_index, 1]
        kspace = jnp.fft.fftn(coil_map * field, norm="ortho")
        tiled = kspace.reshape(NX, SLABS, height, NZ).transpose(1, 0, 2, 3).reshape(SLABS, GRID_TILES, TILE)
        parts = jnp.stack([tiled.real, tiled.imag], 1)
        gridded = lax.map(grid_slab, (slab_weights, slab_bins, counts, parts))
        gridded = gridded.reshape(SLABS, 2, NX, height, NZ).transpose(1, 2, 0, 3, 4).reshape(2, NX, NY, NZ)
        image_back = jnp.fft.ifftn(gridded[0] + 1j * gridded[1], norm="ortho")
        total = total + jnp.conj(coil_map) * image_back
    return jnp.stack([total.real, total.imag]).astype(image.dtype)
```

```python
import functools

import numpy as np
import jax
import jax.numpy as jnp
import ml_dtypes
from jax import lax
from jax.experimental import pallas as pl
from jax.experimental.pallas import tpu as pltpu
from jax.sharding import PartitionSpec as P

N = 256
TILE = 128
SLOTS = 256
CHIPS = 16
RING = 4
PLANES = 8
VMEM_LIMIT = 56 * 1024 * 1024
F32 = jnp.float32
BF16 = jnp.bfloat16


def halves(values):
    high = values.astype(ml_dtypes.bfloat16)
    low = (values - high.astype(np.float64)).astype(ml_dtypes.bfloat16)
    return high, low


def tables():
    index = np.arange(N)
    angle = 2.0 * np.pi * (index[:, None] * index[None, :] % N) / N
    cosine, sine = np.cos(angle) / 16.0, np.sin(angle) / 16.0
    right = np.block([[cosine, -sine], [sine, cosine]])
    left = right.T
    packed = np.arange(2 * N).reshape(2, CHIPS, 2, 8)
    packed = packed.transpose(2, 1, 0, 3).reshape(-1)
    fwd_right = np.concatenate([halves(right)[k] for k in (0, 1, 0)], 0)
    fwd_left = np.concatenate([halves(left)[k] for k in (0, 1, 0)], 1)
    back_left = np.concatenate([halves(right[:, packed])[k] for k in (0, 1, 0)], 1)
    back_right = np.concatenate([halves(left)[k] for k in (0, 1, 0)], 0)
    lanes = []
    for chip in range(CHIPS):
        cos_x = np.repeat(cosine[:, chip * 16 : chip * 16 + 16], 8, axis=1)
        sin_x = np.repeat(sine[:, chip * 16 : chip * 16 + 16], 8, axis=1)
        cos_parts, sin_parts = halves(cos_x), halves(sin_x)
        lanes.append(np.concatenate([cos_parts[0], sin_parts[0], cos_parts[1], sin_parts[1]], 1))
    phases = np.stack(lanes)
    return fwd_right, fwd_left, back_left, back_right, phases, np.ascontiguousarray(phases.transpose(0, 2, 1))


def split(values):
    high = values.astype(BF16)
    low = (values - high.astype(F32)).astype(BF16)
    return high, low


def dot(a, b):
    return lax.dot_general(a, b, (((1,), (0,)), ((), ())), preferred_element_type=F32)


def forward_kernel(image, sens, right, left, out):
    image_re, image_im = image[0, 0], image[1, 0]
    sens_re, sens_im = sens[0, 0, 0], sens[0, 1, 0]
    field = jnp.concatenate(
        [sens_re * image_re - sens_im * image_im, sens_re * image_im + sens_im * image_re], 1
    )
    high, low = split(field)
    field = dot(jnp.concatenate([high, high, low], 1), right[...])
    high, low = split(jnp.concatenate([field[:, :N], field[:, N:]], 0))
    field = dot(left[...], jnp.concatenate([high, high, low], 0))
    field = field.reshape(2, CHIPS, 2, 8, N)
    for part in range(2):
        for core in range(2):
            out[core, :, part, 0] = field[part, :, core]


def forward(image, sens, right, left):
    return pl.pallas_call(
        forward_kernel,
        grid=(PLANES,),
        in_specs=[
            pl.BlockSpec((2, 1, N, N), lambda i: (0, i, 0, 0)),
            pl.BlockSpec((1, 2, 1, N, N), lambda i: (0, 0, i, 0, 0)),
            pl.BlockSpec((6 * N, 2 * N), lambda i: (0, 0)),
            pl.BlockSpec((2 * N, 6 * N), lambda i: (0, 0)),
        ],
        out_specs=pl.BlockSpec((2, CHIPS, 2, 1, 8, N), lambda i: (0, 0, 0, i, 0, 0)),
        out_shape=jax.ShapeDtypeStruct((2, CHIPS, 2, PLANES, 8, N), F32),
        compiler_params=pltpu.CompilerParams(vmem_limit_bytes=VMEM_LIMIT),
        cost_estimate=pl.CostEstimate(flops=6 * 2 * PLANES * 2 * N * 2 * N * N * 2, bytes_accessed=12 << 20, transcendentals=0),
    )(image, sens, right, left)


def place():
    slab = lax.axis_index("slab")
    core = lax.rem(slab, 2)
    chip = slab // 2
    x, y = lax.rem(chip, RING), chip // RING
    return core, chip, x, y


def device(x, y, core):
    return {"slab": (y * RING + x) * 2 + core}


def up(i, step=1):
    return lax.rem(i + step, RING)


def down(i):
    return lax.rem(i + RING - 1, RING)


def meet(peers):
    barrier = pltpu.get_barrier_semaphore()
    for peer in peers:
        pl.semaphore_signal(barrier, inc=1, device_id=peer, device_id_type=pl.DeviceIdType.MESH)
    pl.semaphore_wait(barrier, len(peers))


def remote(src, dst, send, recv, peer):
    return pltpu.make_async_remote_copy(
        src_ref=src, dst_ref=dst, send_sem=send, recv_sem=recv, device_id=peer, device_id_type=pl.DeviceIdType.MESH
    )


class RingSum:
    def __init__(self, src, via_up, via_down, from_down, from_up, send, recv, me, above, below):
        self.src, self.me = src, me
        rows = src.shape[1]
        self.half = (pl.ds(0, rows // 2), pl.ds(rows // 2, rows // 2))
        self.via_up, self.via_down, self.from_down, self.from_up = via_up, via_down, from_down, from_up
        first, second = self.half
        far, near_up, near_down = up(me, 2), up(me), down(me)
        self.copies = [
            remote(src.at[far, first], via_up, send.at[0], recv.at[0], above),
            remote(src.at[far, second], via_down, send.at[1], recv.at[1], below),
            remote(src.at[near_up, second], from_down.at[second], send.at[2], recv.at[2], above),
            remote(src.at[near_down, first], from_up.at[first], send.at[3], recv.at[3], below),
            remote(src.at[near_up, first], from_down.at[first], send.at[4], recv.at[4], above),
            remote(src.at[near_down, second], from_up.at[second], send.at[5], recv.at[5], below),
        ]

    def start(self):
        for copy in self.copies[:4]:
            copy.start()

    def relay(self):
        first, second = self.half
        self.copies[0].wait_recv()
        near = up(self.me)
        self.src[near, first] = self.src[near, first] + self.via_up[...]
        self.copies[4].start()
        self.copies[1].wait_recv()
        near = down(self.me)
        self.src[near, second] = self.src[near, second] + self.via_down[...]
        self.copies[5].start()

    def finish(self, out):
        for k in (2, 3, 4, 5):
            self.copies[k].wait_recv()
        out[...] = self.src[self.me] + self.from_down[...] + self.from_up[...]

    def drain(self):
        for copy in self.copies:
            copy.wait_send()


def scatter_kernel(
    field, bins_col, phases, out,
    both, table, part_a, part_b, mid_a, mid_b,
    va0, va1, va2, va3, vb0, vb1, vb2, vb3, wa0, wa1, wa2, wa3, wb0, wb1, wb2, wb3,
    local_sem, pair_send, pair_recv, send, recv,
):
    core, chip, x, y = place()
    sibling = device(x, y, 1 - core)
    right, left = device(up(x), y, core), device(down(x), y, core)
    above, below = device(x, up(y), core), device(x, down(y), core)
    own = pltpu.make_async_copy(field.at[core], both.at[core], local_sem.at[0])
    own.start()
    fetch = pltpu.make_async_copy(phases.at[chip], table, local_sem.at[1])
    fetch.start()
    meet([sibling, right, left, above, below])
    pair = [
        remote(field.at[1 - core, pl.ds(4 * k, 4)], both.at[core, pl.ds(4 * k, 4)], pair_send.at[k], pair_recv.at[k], sibling)
        for k in range(4)
    ]
    for copy in pair:
        copy.start()
    own.wait()
    fetch.wait()

    def slab_sums(p, carry):
        lane = lax.broadcasted_iota(jnp.int32, (SLOTS, 32), 1)
        bins = jnp.sum(jnp.where(lane == 2 * p + core, bins_col[...], 0.0), axis=1, keepdims=True).astype(jnp.int32)
        kx, ky, side = bins // 16, (bins // 2) % 8, bins % 2
        hot = jnp.where(lax.broadcasted_iota(jnp.int32, (SLOTS, N), 1) == kx, 1.0, 0.0).astype(BF16)
        phase = dot(hot, table[...])
        row = lax.broadcasted_iota(jnp.int32, (SLOTS, 4 * TILE), 1) % 8
        phase = jnp.where(row == ky, phase, 0.0).astype(BF16)
        mats = []
        for k in range(2):
            cosine, sine = phase[:, 2 * k * TILE : (2 * k + 1) * TILE], phase[:, (2 * k + 1) * TILE : (2 * k + 2) * TILE]
            mats.append(jnp.concatenate([jnp.concatenate([cosine, sine], 1), jnp.concatenate([-sine, cosine], 1)], 0))
        rows = jnp.concatenate(
            [both[0, p, 0].reshape(64, N), both[1, p, 0].reshape(64, N), both[0, p, 1].reshape(64, N), both[1, p, 1].reshape(64, N)], 0
        )
        high, low = split(rows)
        sums = dot(jnp.concatenate([mats[0], mats[1], mats[0]], 1), jnp.concatenate([high, high, low], 0))
        sums = jnp.where(jnp.concatenate([side, side], 0) == 0, sums[:, :TILE], sums[:, TILE:])
        px, py = p % RING, p // RING
        part_a[px, pl.ds(py * SLOTS, SLOTS)] = sums[:SLOTS]
        part_b[py, pl.ds(px * SLOTS, SLOTS)] = sums[SLOTS:]
        return carry

    for k in range(4):
        pair[k].wait_recv()
        lax.fori_loop(4 * k, 4 * k + 4, slab_sums, 0)

    a1 = RingSum(part_a, va0, va1, va2, va3, send.at[0], recv.at[0], x, right, left)
    b1 = RingSum(part_b, vb0, vb1, vb2, vb3, send.at[1], recv.at[1], y, above, below)
    a2 = RingSum(mid_a, wa0, wa1, wa2, wa3, send.at[2], recv.at[2], y, above, below)
    b2 = RingSum(mid_b, wb0, wb1, wb2, wb3, send.at[3], recv.at[3], x, right, left)
    a1.start()
    b1.start()
    a1.relay()
    b1.relay()
    a1.finish(part_a.at[x])
    for k in range(RING):
        mid_a[k] = part_a[x, pl.ds(k * SLOTS, SLOTS)]
    a2.start()
    b1.finish(part_b.at[y])
    for k in range(RING):
        mid_b[k] = part_b[y, pl.ds(k * SLOTS, SLOTS)]
    b2.start()
    a2.relay()
    b2.relay()
    a2.finish(out.at[0])
    b2.finish(out.at[1])
    for ring in (a1, b1, a2, b2):
        ring.drain()
    for copy in pair:
        copy.wait_send()


def scatter(field, bins_col, phases):
    big, small = RING * SLOTS, SLOTS
    vias = []
    for rows in (big, big, small, small):
        vias += [pltpu.VMEM((rows // 2, TILE), F32)] * 2 + [pltpu.VMEM((rows, TILE), F32)] * 2
    return pl.pallas_call(
        scatter_kernel,
        out_shape=jax.ShapeDtypeStruct((2, SLOTS, TILE), F32),
        in_specs=[
            pl.BlockSpec(memory_space=pl.ANY),
            pl.BlockSpec(memory_space=pltpu.VMEM),
            pl.BlockSpec(memory_space=pl.ANY),
        ],
        out_specs=pl.BlockSpec(memory_space=pltpu.VMEM),
        scratch_shapes=[
            pltpu.VMEM((2, CHIPS, 2, PLANES, 8, N), F32),
            pltpu.VMEM((N, 4 * TILE), BF16),
            pltpu.VMEM((RING, big, TILE), F32),
            pltpu.VMEM((RING, big, TILE), F32),
            pltpu.VMEM((RING, small, TILE), F32),
            pltpu.VMEM((RING, small, TILE), F32),
        ]
        + vias
        + [
            pltpu.SemaphoreType.DMA((2,)),
            pltpu.SemaphoreType.DMA((4,)),
            pltpu.SemaphoreType.DMA((4,)),
            pltpu.SemaphoreType.DMA((4, 6)),
            pltpu.SemaphoreType.DMA((4, 6)),
        ],
        compiler_params=pltpu.CompilerParams(collective_id=0, has_side_effects=True, vmem_limit_bytes=VMEM_LIMIT),
    )(field, bins_col, phases)


GROUP = 32


def grid_kernel(live, tiles, weights, out):
    row = lax.broadcasted_iota(jnp.int32, (32, TILE), 0) % 8
    base = pl.program_id(0) * GROUP
    for g in range(GROUP // 8):
        rows = pl.ds(8 * g, 8)
        high, low = split(jnp.concatenate([tiles[0, rows], tiles[1, rows]], 0))
        mat = weights[rows].reshape(8 * TILE, TILE)
        spread = lax.dot_general(
            jnp.concatenate([high, low], 0), mat, (((1,), (1,)), ((), ())), preferred_element_type=F32
        )
        samples = jnp.zeros((32, TILE), F32)
        for j in range(8):
            samples = jnp.where(row == j, spread[:, j * TILE : (j + 1) * TILE], samples)
        samples = samples[:16] + samples[16:]
        high = samples.astype(BF16).astype(F32)
        both = jnp.concatenate([high, samples - high], 0)
        masked = jnp.concatenate([jnp.where(row == j, both, 0.0).astype(BF16) for j in range(8)], 1)
        back = dot(masked, mat)
        back = back[:16] + back[16:]
        slot = base + 8 * g + lax.broadcasted_iota(jnp.int32, (16, TILE), 0) % 8
        back = jnp.where(slot < live[0], back, 0.0)
        out[0, rows] = back[:8]
        out[1, rows] = back[8:]


def grid(live, tiles, weights):
    return pl.pallas_call(
        grid_kernel,
        grid=(SLOTS // GROUP,),
        in_specs=[
            pl.BlockSpec(memory_space=pltpu.SMEM),
            pl.BlockSpec((2, GROUP, TILE), lambda i: (0, i, 0)),
            pl.BlockSpec((GROUP, TILE, TILE), lambda i: (i, 0, 0)),
        ],
        out_specs=pl.BlockSpec((2, GROUP, TILE), lambda i: (0, i, 0)),
        out_shape=jax.ShapeDtypeStruct((2, SLOTS, TILE), F32),
        compiler_params=pltpu.CompilerParams(vmem_limit_bytes=VMEM_LIMIT),
    )(live, tiles, weights)


class RingGather:
    def __init__(self, buf, send, recv, me, above, below):
        rows = buf.shape[1]
        first, second = pl.ds(0, rows // 2), pl.ds(rows // 2, rows // 2)
        near_down, near_up, far = down(me), up(me), up(me, 2)
        self.copies = [
            remote(buf.at[me], buf.at[me], send.at[0], recv.at[0], above),
            remote(buf.at[me], buf.at[me], send.at[1], recv.at[1], below),
            remote(buf.at[near_down, first], buf.at[near_down, first], send.at[2], recv.at[2], above),
            remote(buf.at[near_up, second], buf.at[near_up, second], send.at[3], recv.at[3], below),
        ]

    def start(self):
        self.copies[0].start()
        self.copies[1].start()

    def relay(self):
        self.copies[0].wait_recv()
        self.copies[2].start()
        self.copies[1].wait_recv()
        self.copies[3].start()

    def finish(self):
        self.copies[2].wait_recv()
        self.copies[3].wait_recv()

    def drain(self):
        for copy in self.copies:
            copy.wait_send()


def gather_kernel(
    back, bins_row, bins_col, phases, left, right, sens, out,
    all_a, all_b, mid_a, mid_b, table, sens_buf, plane, outgoing, term, via_up, via_down, from_down, from_up,
    local_sem, send, recv, pair_send, pair_recv, coil_send, coil_recv,
):
    core, chip, x, y = place()
    coil = lax.axis_index("coil")
    sibling = device(x, y, 1 - core)
    east, west = device(up(x), y, core), device(down(x), y, core)
    north, south = device(x, up(y), core), device(x, down(y), core)
    over, under = {"coil": up(coil)}, {"coil": down(coil)}
    fetch = pltpu.make_async_copy(phases.at[chip], table, local_sem.at[0])
    fetch.start()
    fetch_sens = pltpu.make_async_copy(sens.at[0], sens_buf, local_sem.at[1])
    fetch_sens.start()
    mid_a[y] = back[0]
    mid_b[x] = back[1]
    meet([sibling, east, west, north, south, over, under])

    a1 = RingGather(mid_a, send.at[0], recv.at[0], y, north, south)
    b1 = RingGather(mid_b, send.at[1], recv.at[1], x, east, west)
    a2 = RingGather(all_a, send.at[2], recv.at[2], x, east, west)
    b2 = RingGather(all_b, send.at[3], recv.at[3], y, north, south)
    a1.start()
    b1.start()
    a1.relay()
    b1.relay()
    a1.finish()
    for k in range(RING):
        all_a[x, pl.ds(k * SLOTS, SLOTS)] = mid_a[k]
    a2.start()
    b1.finish()
    for k in range(RING):
        all_b[y, pl.ds(k * SLOTS, SLOTS)] = mid_b[k]
    b2.start()
    a2.relay()
    b2.relay()
    fetch.wait()
    a2.finish()
    b2.finish()

    def slab_sums(p, carry):
        lane = lax.broadcasted_iota(jnp.int32, (SLOTS, 32), 1)
        column = jnp.sum(jnp.where(lane == 2 * p + core, bins_col[...], 0.0), axis=1, keepdims=True).astype(jnp.int32)
        side = column % 2
        bins = bins_row[pl.ds(2 * p + core, 1), :].astype(jnp.int32)
        kx, ky = bins // 16, (bins // 2) % 8
        hot = jnp.where(lax.broadcasted_iota(jnp.int32, (N, SLOTS), 0) == kx, 1.0, 0.0).astype(BF16)
        phase = dot(table[...], hot)
        row = lax.broadcasted_iota(jnp.int32, (4 * TILE, SLOTS), 0) % 8
        phase = jnp.where(row == ky, phase, 0.0).astype(BF16)
        mats = []
        for k in range(2):
            cosine, sine = phase[2 * k * TILE : (2 * k + 1) * TILE], phase[(2 * k + 1) * TILE : (2 * k + 2) * TILE]
            mats.append(jnp.concatenate([jnp.concatenate([cosine, -sine], 1), jnp.concatenate([sine, cosine], 1)], 0))
        px, py = p % RING, p // RING
        tiles = jnp.concatenate([all_a[px, pl.ds(py * SLOTS, SLOTS)], all_b[py, pl.ds(px * SLOTS, SLOTS)]], 0)
        side = jnp.concatenate([side, side], 0)
        tiles = jnp.concatenate([jnp.where(side == 0, tiles, 0.0), jnp.where(side == 1, tiles, 0.0)], 1)
        high, low = split(tiles)
        sums = dot(jnp.concatenate([mats[0], mats[1], mats[0]], 1), jnp.concatenate([high, high, low], 0))
        sums = sums.reshape(2, 2, PLANES, 8, N)
        lower, upper = sums[:, 0], sums[:, 1]
        mine = jnp.where(core == 0, lower, upper)
        other = jnp.where(core == 0, upper, lower)
        for part in range(2):
            plane[:, core, p, part] = mine[part]
            outgoing[:, p, part] = other[part]
        return carry

    lax.fori_loop(0, CHIPS, slab_sums, 0)
    pair = [remote(outgoing.at[i], plane.at[i, core], pair_send.at[i], pair_recv.at[i], sibling) for i in range(PLANES)]
    for copy in pair:
        copy.start()
    fetch_sens.wait()

    far, near_up, near_down = up(coil, 2), up(coil), down(coil)

    def coil_copies(i):
        s, r = coil_send.at[i], coil_recv.at[i]
        return [
            remote(term.at[i, far, 0], via_up.at[i], s.at[0], r.at[0], over),
            remote(term.at[i, far, 1], via_down.at[i], s.at[1], r.at[1], under),
            remote(term.at[i, near_up, 1], from_down.at[i, 1], s.at[2], r.at[2], over),
            remote(term.at[i, near_down, 0], from_up.at[i, 0], s.at[3], r.at[3], under),
            remote(term.at[i, near_up, 0], from_down.at[i, 0], s.at[4], r.at[4], over),
            remote(term.at[i, near_down, 1], from_up.at[i, 1], s.at[5], r.at[5], under),
        ]

    def relay(i):
        copies = coil_copies(i)
        copies[0].wait_recv()
        term[i, near_up, 0] = term[i, near_up, 0] + via_up[i]
        copies[4].start()
        copies[1].wait_recv()
        term[i, near_down, 1] = term[i, near_down, 1] + via_down[i]
        copies[5].start()

    def plane_back(i, carry):
        remote(outgoing.at[i], plane.at[i, core], pair_send.at[i], pair_recv.at[i], sibling).wait_recv()
        high, low = split(plane[i].reshape(2 * N, N))
        field = dot(left[...], jnp.concatenate([high, high, low], 0))
        high, low = split(jnp.concatenate([field[:N], field[N:]], 1))
        field = dot(jnp.concatenate([high, high, low], 1), right[...])
        field_re, field_im = field[:, :N], field[:, N:]
        sens_re, sens_im = sens_buf[0, i], sens_buf[1, i]
        term[i, :, 0] = (sens_re * field_re + sens_im * field_im).reshape(RING, N // RING, N)
        term[i, :, 1] = (sens_re * field_im - sens_im * field_re).reshape(RING, N // RING, N)
        for copy in coil_copies(i)[:4]:
            copy.start()

        @pl.when(i > 0)
        def _():
            relay(i - 1)

        return carry

    lax.fori_loop(0, PLANES, plane_back, 0)
    relay(PLANES - 1)

    def collect(i, carry):
        copies = coil_copies(i)
        for k in (2, 3, 4, 5):
            copies[k].wait_recv()
        total = term[i, coil] + from_down[i] + from_up[i]
        for part in range(2):
            out[part, i] = total[part]
        for copy in copies:
            copy.wait_send()
        return carry

    lax.fori_loop(0, PLANES, collect, 0)
    for ring in (a1, b1, a2, b2):
        ring.drain()
    for copy in pair:
        copy.wait_send()


def gather(back, bins_row, bins_col, phases, left, right, sens):
    quarter = N // RING
    vmem = pl.BlockSpec(memory_space=pltpu.VMEM)
    hbm = pl.BlockSpec(memory_space=pl.ANY)
    return pl.pallas_call(
        gather_kernel,
        out_shape=jax.ShapeDtypeStruct((2, PLANES, quarter, N), F32),
        in_specs=[vmem, vmem, vmem, hbm, vmem, vmem, hbm],
        out_specs=vmem,
        scratch_shapes=[
            pltpu.VMEM((RING, RING * SLOTS, TILE), F32),
            pltpu.VMEM((RING, RING * SLOTS, TILE), F32),
            pltpu.VMEM((RING, SLOTS, TILE), F32),
            pltpu.VMEM((RING, SLOTS, TILE), F32),
            pltpu.VMEM((4 * TILE, N), BF16),
            pltpu.VMEM((2, PLANES, N, N), F32),
            pltpu.VMEM((PLANES, 2, CHIPS, 2, 8, N), F32),
            pltpu.VMEM((PLANES, CHIPS, 2, 8, N), F32),
            pltpu.VMEM((PLANES, RING, 2, quarter, N), F32),
            pltpu.VMEM((PLANES, quarter, N), F32),
            pltpu.VMEM((PLANES, quarter, N), F32),
            pltpu.VMEM((PLANES, 2, quarter, N), F32),
            pltpu.VMEM((PLANES, 2, quarter, N), F32),
            pltpu.SemaphoreType.DMA((2,)),
            pltpu.SemaphoreType.DMA((4, 4)),
            pltpu.SemaphoreType.DMA((4, 4)),
            pltpu.SemaphoreType.DMA((PLANES,)),
            pltpu.SemaphoreType.DMA((PLANES,)),
            pltpu.SemaphoreType.DMA((PLANES, 6)),
            pltpu.SemaphoreType.DMA((PLANES, 6)),
        ],
        compiler_params=pltpu.CompilerParams(collective_id=1, has_side_effects=True, vmem_limit_bytes=VMEM_LIMIT),
    )(back, bins_row, bins_col, phases, left, right, sens)


def body(image, sens, weights, bins, counts):
    fwd_right, fwd_left, back_left, back_right, phases, phases_t = (jnp.asarray(t) for t in tables())
    bins_row = lax.all_gather(bins, "slab").astype(F32)
    bins_col = bins_row.T
    field = forward(image, sens, fwd_right, fwd_left)
    tiles = scatter(field, bins_col, phases)
    back = grid(counts, tiles, weights)
    return gather(back, bins_row, bins_col, phases_t, back_left, back_right, sens)


def solution(mesh):
    in_specs = (
        P(None, "slab", None, None),
        P("coil", None, "slab", None, None),
        P("slab", None, None),
        P("slab"),
        P("slab"),
    )
    out_specs = P(None, "slab", "coil", None)
    return jax.shard_map(body, mesh=mesh, in_specs=in_specs, out_specs=out_specs, check_vma=False)
```

```python
import functools

import numpy as np
import jax
import jax.numpy as jnp
import ml_dtypes
from jax import lax
from jax.experimental import pallas as pl
from jax.experimental.pallas import tpu as pltpu
from jax.sharding import PartitionSpec as P

N = 256
TILE = 128
SLOTS = 256
CHIPS = 16
RING = 4
PLANES = 8
GROUP = 32
VMEM_LIMIT = 56 * 1024 * 1024
F32 = jnp.float32
BF16 = jnp.bfloat16


def halves(values):
    high = values.astype(ml_dtypes.bfloat16)
    low = (values - high.astype(np.float64)).astype(ml_dtypes.bfloat16)
    return high, low


def stack(table, axis):
    high, low = halves(table)
    return np.concatenate([high, low, high], axis)


def wave(rows, columns):
    angle = 2.0 * np.pi * (rows[:, None] * columns[None, :] % N) / N
    return np.cos(angle) / 16.0, np.sin(angle) / 16.0


EVEN = 2 * np.arange(TILE)
ODD = (2 * np.arange(TILE) + 1 + TILE) % N


def tables():
    first = np.arange(TILE)
    fwd_right, fwd_left, back_left, back_right = [], [], [], []
    packed = np.arange(2 * TILE).reshape(2, PLANES, 2, 8).transpose(2, 1, 0, 3).reshape(-1)
    for odd in range(2):
        cosine, sine = wave(first, (EVEN, ODD)[odd])
        fwd_right.append(stack(np.block([[cosine, -sine], [sine, cosine]]), 0))
        cosine, sine = wave((EVEN, ODD)[odd], first)
        back_right.append(stack(np.block([[cosine, sine], [-sine, cosine]]), 0))
        cosine, sine = wave(first, 2 * first + odd)
        fwd_left.append(stack(np.block([[cosine, sine], [-sine, cosine]]), 1))
        cosine, sine = wave(2 * first + odd, first)
        back_left.append(stack(np.block([[cosine, -sine], [sine, cosine]])[:, packed], 1))
    lanes = []
    cosine, sine = wave(np.arange(N), np.arange(N))
    for chip in range(CHIPS):
        cos_x = np.repeat(cosine[:, chip * 16 : chip * 16 + 16], 8, axis=1)
        sin_x = np.repeat(sine[:, chip * 16 : chip * 16 + 16], 8, axis=1)
        cos_parts, sin_parts = halves(cos_x), halves(sin_x)
        lanes.append(np.concatenate([cos_parts[0], sin_parts[0], cos_parts[1], sin_parts[1]], 1))
    phases = np.stack(lanes)
    lane = np.arange(TILE)
    order = np.stack([np.where(lane < 64, 2 * lane, 2 * lane - TILE + 1), np.where(lane < 64, 2 * lane + 1, 2 * lane - TILE)])
    natural = np.concatenate([np.eye(TILE)[order[0]], np.eye(TILE)[order[1]]], 0).astype(ml_dtypes.bfloat16)
    return {
        "fwd_right": np.stack(fwd_right),
        "fwd_left": np.stack(fwd_left),
        "back_left": np.stack(back_left),
        "back_right": np.stack(back_right),
        "phases": phases,
        "phases_t": np.ascontiguousarray(phases.transpose(0, 2, 1)),
        "natural": natural,
        "packed": np.ascontiguousarray(natural.T),
    }


def split(values):
    high = values.astype(BF16)
    low = (values - high.astype(F32)).astype(BF16)
    return high, low


def dot(a, b):
    return lax.dot_general(a, b, (((1,), (0,)), ((), ())), preferred_element_type=F32)


def wide(values):
    high, low = split(values)
    return jnp.concatenate([high, high, low], 1)


def tall(values):
    high, low = split(values)
    return jnp.concatenate([high, high, low], 0)


def place():
    slab = lax.axis_index("slab")
    core = lax.rem(slab, 2)
    chip = slab // 2
    x, y = lax.rem(chip, RING), chip // RING
    return core, chip, x, y


def device(x, y, core):
    return {"slab": (y * RING + x) * 2 + core}


def up(i, step=1):
    return lax.rem(i + step, RING)


def down(i):
    return lax.rem(i + RING - 1, RING)


def halved(source, target, sem, i, first):
    return [
        pltpu.make_async_copy(source.at[:, i, :, pl.ds(half * TILE, TILE)], target.at[:, i, half], sem.at[i, first + half])
        for half in range(2)
    ]


def meet(peers):
    barrier = pltpu.get_barrier_semaphore()
    for peer in peers:
        pl.semaphore_signal(barrier, inc=1, device_id=peer, device_id_type=pl.DeviceIdType.MESH)
    pl.semaphore_wait(barrier, len(peers))


def remote(src, dst, send, recv, peer):
    return pltpu.make_async_remote_copy(
        src_ref=src, dst_ref=dst, send_sem=send, recv_sem=recv, device_id=peer, device_id_type=pl.DeviceIdType.MESH
    )


class RingSum:
    def __init__(self, src, via_up, via_down, from_down, from_up, send, recv, me, above, below):
        self.src, self.me = src, me
        rows = src.shape[1]
        self.half = (pl.ds(0, rows // 2), pl.ds(rows // 2, rows // 2))
        self.via_up, self.via_down, self.from_down, self.from_up = via_up, via_down, from_down, from_up
        first, second = self.half
        far, near_up, near_down = up(me, 2), up(me), down(me)
        self.copies = [
            remote(src.at[far, first], via_up, send.at[0], recv.at[0], above),
            remote(src.at[far, second], via_down, send.at[1], recv.at[1], below),
            remote(src.at[near_up, second], from_down.at[second], send.at[2], recv.at[2], above),
            remote(src.at[near_down, first], from_up.at[first], send.at[3], recv.at[3], below),
            remote(src.at[near_up, first], from_down.at[first], send.at[4], recv.at[4], above),
            remote(src.at[near_down, second], from_up.at[second], send.at[5], recv.at[5], below),
        ]

    def start_far(self):
        for copy in self.copies[:2]:
            copy.start()

    def start_near(self):
        for copy in self.copies[2:4]:
            copy.start()

    def relay(self):
        first, second = self.half
        self.copies[0].wait_recv()
        near = up(self.me)
        self.src[near, first] = self.src[near, first] + self.via_up[...]
        self.copies[4].start()
        self.copies[1].wait_recv()
        near = down(self.me)
        self.src[near, second] = self.src[near, second] + self.via_down[...]
        self.copies[5].start()

    def finish(self, out):
        for k in (2, 3, 4, 5):
            self.copies[k].wait_recv()
        out[...] = self.src[self.me] + self.from_down[...] + self.from_up[...]

    def drain(self):
        for copy in self.copies:
            copy.wait_send()


def scatter_kernel(
    image, sens, bins, fwd_right, fwd_left, phases, out, bins_row, bins_col, side_out,
    image_buf, sens_buf, field, table, part_a, part_b, mid_a, mid_b,
    va0, va1, va2, va3, vb0, vb1, vb2, vb3, wa0, wa1, wa2, wa3, wb0, wb1, wb2, wb3,
    load_sem, table_sem, bin_send, bin_recv, pair_send, pair_recv, send, recv,
):
    core, chip, x, y = place()
    sibling = device(x, y, 1 - core)
    right, left = device(up(x), y, core), device(down(x), y, core)
    above, below = device(x, up(y), core), device(x, down(y), core)

    def loads(i):
        return halved(image, image_buf, load_sem, i, 0) + halved(sens.at[0], sens_buf, load_sem, i, 2)

    def start_load(i, carry):
        for copy in loads(i):
            copy.start()
        return carry

    lax.fori_loop(0, PLANES, start_load, 0)
    fetch = pltpu.make_async_copy(phases.at[chip], table, table_sem)
    fetch.start()
    bins_row[chip] = jnp.broadcast_to(bins[...].astype(F32), (8, SLOTS))
    others = [{"slab": lax.rem(chip + k, CHIPS) * 2 + core} for k in range(1, CHIPS)]
    meet([sibling] + others)
    spread = [remote(bins_row.at[chip], bins_row.at[chip], bin_send.at[k], bin_recv.at[k], others[k]) for k in range(CHIPS - 1)]
    for copy in spread:
        copy.start()

    def pair(i):
        return remote(field.at[2, i], field.at[core, i], pair_send.at[i], pair_recv.at[i], sibling)

    def plane(i, carry):
        for copy in loads(i):
            copy.wait()
        summed, differed = [], []
        for odd in range(2):
            rows = pl.ds(odd, TILE, stride=2)
            parts = []
            for half in range(2):
                image_re, image_im = image_buf[0, i, half, rows, :], image_buf[1, i, half, rows, :]
                sens_re, sens_im = sens_buf[0, i, half, rows, :], sens_buf[1, i, half, rows, :]
                parts.append((sens_re * image_re - sens_im * image_im, sens_re * image_im + sens_im * image_re))
            summed.append(jnp.concatenate([parts[0][k] + parts[1][k] for k in range(2)], 1))
            differed.append(jnp.concatenate([parts[0][k] - parts[1][k] for k in range(2)], 1))
        even_z = dot(wide(jnp.concatenate(summed, 0)), fwd_right[0])
        odd_z = dot(wide(jnp.concatenate(differed, 0)), fwd_right[1])
        parts = []
        for odd in range(2):
            rows = slice(odd * TILE, (odd + 1) * TILE)
            stacked = jnp.concatenate(
                [
                    jnp.concatenate([even_z[rows, :TILE], odd_z[rows, :TILE]], 1),
                    jnp.concatenate([even_z[rows, TILE:], odd_z[rows, TILE:]], 1),
                ],
                0,
            )
            parts.append(dot(fwd_left[odd], tall(stacked)))
        for side, values in enumerate((parts[0] + parts[1], parts[0] - parts[1])):
            values = values.reshape(2, 8, 2, 8, N)
            for part in range(2):
                field[2 * core, i, pl.ds(8 * side, 8), part] = values[part, :, 0]
                field[2 - core, i, pl.ds(8 * side, 8), part] = values[part, :, 1]
        pair(i).start()
        return carry

    lax.fori_loop(0, PLANES, plane, 0)
    fetch.wait()
    for copy in spread:
        copy.wait_recv()
    bins_col[...] = bins_row[...].reshape(CHIPS * 8, SLOTS).T
    lane = lax.broadcasted_iota(jnp.int32, (SLOTS, TILE), 1)

    def column(p):
        return jnp.sum(jnp.where(lane == 8 * p, bins_col[...], 0.0), axis=1, keepdims=True).astype(jnp.int32)

    side_out[...] = jnp.broadcast_to((column(chip) % 2).astype(F32), (SLOTS, TILE))

    def slab_sums(px, py):
        p = py * RING + px
        bins = column(p)
        kx, ky, side = bins // 16, (bins // 2) % 8, bins % 2
        hot = jnp.where(lax.broadcasted_iota(jnp.int32, (SLOTS, N), 1) == kx, 1.0, 0.0).astype(BF16)
        phase = dot(hot, table[...])
        row = lax.broadcasted_iota(jnp.int32, (SLOTS, 4 * TILE), 1) % 8
        phase = jnp.where(row == ky, phase, 0.0).astype(BF16)
        mats = []
        for k in range(2):
            cosine, sine = phase[:, 2 * k * TILE : (2 * k + 1) * TILE], phase[:, (2 * k + 1) * TILE : (2 * k + 2) * TILE]
            mats.append(jnp.concatenate([jnp.concatenate([cosine, sine], 1), jnp.concatenate([-sine, cosine], 1)], 0))
        rows = jnp.concatenate([field[c, :, p, part].reshape(64, N) for part in range(2) for c in range(2)], 0)
        sums = dot(jnp.concatenate([mats[0], mats[1], mats[0]], 1), tall(rows))
        low_lane = jnp.where(lane < 64, 0, 1) == side
        part_a[px, pl.ds(py * SLOTS, SLOTS)] = jnp.where(low_lane, sums[:SLOTS, :TILE], sums[:SLOTS, TILE:])
        part_b[py, pl.ds(px * SLOTS, SLOTS)] = jnp.where(low_lane, sums[SLOTS:, :TILE], sums[SLOTS:, TILE:])

    def far_column(k, carry):
        slab_sums(up(x, 2), up(y, k))
        return carry

    def far_row(k, carry):
        slab_sums(up(x, 3 + k), up(y, 2))
        return carry

    def near(k, carry):
        m = k + k // 4
        slab_sums(up(x, 3 + m % 3), up(y, 3 + m // 3))
        return carry

    a1 = RingSum(part_a, va0, va1, va2, va3, send.at[0], recv.at[0], x, right, left)
    b1 = RingSum(part_b, vb0, vb1, vb2, vb3, send.at[1], recv.at[1], y, above, below)
    a2 = RingSum(mid_a, wa0, wa1, wa2, wa3, send.at[2], recv.at[2], y, above, below)
    b2 = RingSum(mid_b, wb0, wb1, wb2, wb3, send.at[3], recv.at[3], x, right, left)

    def arrived(i, carry):
        pair(i).wait_recv()
        return carry

    lax.fori_loop(0, PLANES, arrived, 0)
    lax.fori_loop(0, 4, far_column, 0, unroll=2)
    lax.fori_loop(0, 3, far_row, 0, unroll=3)
    a1.start_far()
    b1.start_far()
    lax.fori_loop(0, 8, near, 0, unroll=2)
    a1.start_near()
    b1.start_near()
    slab_sums(x, y)
    a1.relay()
    b1.relay()
    a1.finish(part_a.at[x])
    for k in range(RING):
        mid_a[k] = part_a[x, pl.ds(k * SLOTS, SLOTS)]
    a2.start_far()
    a2.start_near()
    b1.finish(part_b.at[y])
    for k in range(RING):
        mid_b[k] = part_b[y, pl.ds(k * SLOTS, SLOTS)]
    b2.start_far()
    b2.start_near()
    a2.relay()
    b2.relay()
    a2.finish(out.at[0])
    b2.finish(out.at[1])
    for ring in (a1, b1, a2, b2):
        ring.drain()
    for copy in spread:
        copy.wait_send()

    def sent(i, carry):
        pair(i).wait_send()
        return carry

    lax.fori_loop(0, PLANES, sent, 0)


def scatter(image, sens, bins, tab):
    big, small = RING * SLOTS, SLOTS
    vias = []
    for rows in (big, big, small, small):
        vias += [pltpu.VMEM((rows // 2, TILE), F32)] * 2 + [pltpu.VMEM((rows, TILE), F32)] * 2
    vmem = pl.BlockSpec(memory_space=pltpu.VMEM)
    hbm = pl.BlockSpec(memory_space=pl.ANY)
    return pl.pallas_call(
        scatter_kernel,
        out_shape=(
            jax.ShapeDtypeStruct((2, SLOTS, TILE), F32),
            jax.ShapeDtypeStruct((CHIPS, 8, SLOTS), F32),
            jax.ShapeDtypeStruct((SLOTS, CHIPS * 8), F32),
            jax.ShapeDtypeStruct((SLOTS, TILE), F32),
        ),
        in_specs=[hbm, hbm, vmem, vmem, vmem, hbm],
        out_specs=(vmem, vmem, vmem, vmem),
        scratch_shapes=[
            pltpu.VMEM((2, PLANES, 2, N, TILE), F32),
            pltpu.VMEM((2, PLANES, 2, N, TILE), F32),
            pltpu.VMEM((3, PLANES, CHIPS, 2, 8, N), F32),
            pltpu.VMEM((N, 4 * TILE), BF16),
            pltpu.VMEM((RING, big, TILE), F32),
            pltpu.VMEM((RING, big, TILE), F32),
            pltpu.VMEM((RING, small, TILE), F32),
            pltpu.VMEM((RING, small, TILE), F32),
        ]
        + vias
        + [
            pltpu.SemaphoreType.DMA((PLANES, 4)),
            pltpu.SemaphoreType.DMA,
            pltpu.SemaphoreType.DMA((CHIPS - 1,)),
            pltpu.SemaphoreType.DMA((CHIPS - 1,)),
            pltpu.SemaphoreType.DMA((PLANES,)),
            pltpu.SemaphoreType.DMA((PLANES,)),
            pltpu.SemaphoreType.DMA((4, 6)),
            pltpu.SemaphoreType.DMA((4, 6)),
        ],
        compiler_params=pltpu.CompilerParams(collective_id=0, has_side_effects=True, vmem_limit_bytes=VMEM_LIMIT),
    )(image, sens, bins, tab["fwd_right"], tab["fwd_left"], tab["phases"])


def grid_kernel(live, tiles, side, weights, natural, packed, out):
    row = lax.broadcasted_iota(jnp.int32, (32, TILE), 0) % 8
    base = pl.program_id(0) * GROUP
    for g in range(GROUP // 8):
        rows = pl.ds(8 * g, 8)
        upper = jnp.concatenate([side[rows]] * 4, 0) == 1.0
        values = jnp.concatenate([tiles[0, rows], tiles[1, rows]], 0)
        high = values.astype(BF16).astype(F32)
        both = jnp.concatenate([high, values - high], 0)
        both = jnp.concatenate([jnp.where(upper, 0.0, both), jnp.where(upper, both, 0.0)], 1).astype(BF16)
        mat = weights[rows].reshape(8 * TILE, TILE)
        spread = lax.dot_general(
            dot(both, natural[...]).astype(BF16), mat, (((1,), (1,)), ((), ())), preferred_element_type=F32
        )
        samples = jnp.zeros((32, TILE), F32)
        for j in range(8):
            samples = jnp.where(row == j, spread[:, j * TILE : (j + 1) * TILE], samples)
        samples = samples[:16] + samples[16:]
        high = samples.astype(BF16).astype(F32)
        both = jnp.concatenate([high, samples - high], 0)
        masked = jnp.concatenate([jnp.where(row == j, both, 0.0).astype(BF16) for j in range(8)], 1)
        back = dot(masked, mat)
        back = back[:16] + back[16:]
        high, low = split(back)
        back = dot(jnp.concatenate([high, low], 0), packed[...])
        back = jnp.where(upper, back[:, TILE:], back[:, :TILE])
        back = back[:16] + back[16:]
        slot = base + 8 * g + lax.broadcasted_iota(jnp.int32, (16, TILE), 0) % 8
        back = jnp.where(slot < live[0], back, 0.0)
        out[0, rows] = back[:8]
        out[1, rows] = back[8:]


def grid(live, tiles, side, weights, tab):
    return pl.pallas_call(
        grid_kernel,
        grid=(SLOTS // GROUP,),
        in_specs=[
            pl.BlockSpec(memory_space=pltpu.SMEM),
            pl.BlockSpec((2, GROUP, TILE), lambda i: (0, i, 0)),
            pl.BlockSpec((GROUP, TILE), lambda i: (i, 0)),
            pl.BlockSpec((GROUP, TILE, TILE), lambda i: (i, 0, 0)),
            pl.BlockSpec((2 * TILE, TILE), lambda i: (0, 0)),
            pl.BlockSpec((TILE, 2 * TILE), lambda i: (0, 0)),
        ],
        out_specs=pl.BlockSpec((2, GROUP, TILE), lambda i: (0, i, 0)),
        out_shape=jax.ShapeDtypeStruct((2, SLOTS, TILE), F32),
        compiler_params=pltpu.CompilerParams(vmem_limit_bytes=VMEM_LIMIT),
    )(live, tiles, side, weights, tab["natural"], tab["packed"])


class RingGather:
    def __init__(self, buf, send, recv, me, above, below):
        rows = buf.shape[1]
        first, second = pl.ds(0, rows // 2), pl.ds(rows // 2, rows // 2)
        near_down, near_up, far = down(me), up(me), up(me, 2)
        self.copies = [
            remote(buf.at[me], buf.at[me], send.at[0], recv.at[0], above),
            remote(buf.at[me], buf.at[me], send.at[1], recv.at[1], below),
            remote(buf.at[near_down, first], buf.at[near_down, first], send.at[2], recv.at[2], above),
            remote(buf.at[near_up, second], buf.at[near_up, second], send.at[3], recv.at[3], below),
        ]

    def start(self):
        self.copies[0].start()
        self.copies[1].start()

    def relay(self):
        self.copies[0].wait_recv()
        self.copies[2].start()
        self.copies[1].wait_recv()
        self.copies[3].start()

    def finish(self):
        self.copies[2].wait_recv()
        self.copies[3].wait_recv()

    def drain(self):
        for copy in self.copies:
            copy.wait_send()


def gather_kernel(
    back, bins_row, bins_col, phases, left, right, sens, out,
    all_a, all_b, mid_a, mid_b, table, sens_buf, plane, outgoing, term, via_up, via_down, from_down, from_up, result,
    local_sem, sens_sem, send, recv, pair_send, pair_recv, coil_send, coil_recv,
):
    core, chip, x, y = place()
    coil = lax.axis_index("coil")
    sibling = device(x, y, 1 - core)
    east, west = device(up(x), y, core), device(down(x), y, core)
    north, south = device(x, up(y), core), device(x, down(y), core)
    over, under = {"coil": up(coil)}, {"coil": down(coil)}
    fetch = pltpu.make_async_copy(phases.at[chip], table, local_sem.at[0])
    fetch.start()

    def load_sens(i, carry):
        for copy in halved(sens.at[0], sens_buf, sens_sem, i, 0):
            copy.start()
        return carry

    lax.fori_loop(0, PLANES, load_sens, 0)
    mid_a[y] = back[0]
    mid_b[x] = back[1]
    meet([sibling, east, west, north, south, over, under])

    a1 = RingGather(mid_a, send.at[0], recv.at[0], y, north, south)
    b1 = RingGather(mid_b, send.at[1], recv.at[1], x, east, west)
    a2 = RingGather(all_a, send.at[2], recv.at[2], x, east, west)
    b2 = RingGather(all_b, send.at[3], recv.at[3], y, north, south)
    a1.start()
    b1.start()
    a1.relay()
    b1.relay()
    a1.finish()
    for k in range(RING):
        all_a[x, pl.ds(k * SLOTS, SLOTS)] = mid_a[k]
    a2.start()
    b1.finish()
    for k in range(RING):
        all_b[y, pl.ds(k * SLOTS, SLOTS)] = mid_b[k]
    b2.start()
    a2.relay()
    b2.relay()
    fetch.wait()
    a2.finish()
    b2.finish()

    def slab_sums(p, carry):
        lane = lax.broadcasted_iota(jnp.int32, (SLOTS, TILE), 1)
        column = jnp.sum(jnp.where(lane == 8 * p, bins_col[...], 0.0), axis=1, keepdims=True).astype(jnp.int32)
        side = column % 2
        bins = bins_row[p, 0:1, :].astype(jnp.int32)
        kx, ky = bins // 16, (bins // 2) % 8
        hot = jnp.where(lax.broadcasted_iota(jnp.int32, (N, SLOTS), 0) == kx, 1.0, 0.0).astype(BF16)
        phase = dot(table[...], hot)
        row = lax.broadcasted_iota(jnp.int32, (4 * TILE, SLOTS), 0) % 8
        phase = jnp.where(row == ky, phase, 0.0).astype(BF16)
        mats = []
        for k in range(2):
            cosine, sine = phase[2 * k * TILE : (2 * k + 1) * TILE], phase[(2 * k + 1) * TILE : (2 * k + 2) * TILE]
            mats.append(jnp.concatenate([jnp.concatenate([cosine, -sine], 1), jnp.concatenate([sine, cosine], 1)], 0))
        px, py = p % RING, p // RING
        tiles = jnp.concatenate([all_a[px, pl.ds(py * SLOTS, SLOTS)], all_b[py, pl.ds(px * SLOTS, SLOTS)]], 0)
        low_lane = jnp.where(lane < 64, 0, 1) == side
        low_lane = jnp.concatenate([low_lane, low_lane], 0)
        tiles = jnp.concatenate([jnp.where(low_lane, tiles, 0.0), jnp.where(low_lane, 0.0, tiles)], 1)
        sums = dot(jnp.concatenate([mats[0], mats[1], mats[0]], 1), tall(tiles))
        sums = sums.reshape(2, 2, PLANES, 8, N)
        lower, upper = sums[:, 0], sums[:, 1]
        mine = jnp.where(core == 0, lower, upper)
        other = jnp.where(core == 0, upper, lower)
        for part in range(2):
            plane[:, core, p, part] = mine[part]
            outgoing[:, p, part] = other[part]
        return carry

    lax.fori_loop(0, CHIPS, slab_sums, 0)
    pair = [remote(outgoing.at[i], plane.at[i, core], pair_send.at[i], pair_recv.at[i], sibling) for i in range(PLANES)]
    for copy in pair:
        copy.start()

    far, near_up, near_down = up(coil, 2), up(coil), down(coil)

    def coil_copies(i):
        s, r = coil_send.at[i], coil_recv.at[i]
        return [
            remote(term.at[i, far, 0], via_up.at[i], s.at[0], r.at[0], over),
            remote(term.at[i, far, 1], via_down.at[i], s.at[1], r.at[1], under),
            remote(term.at[i, near_up, 1], from_down.at[i, 1], s.at[2], r.at[2], over),
            remote(term.at[i, near_down, 0], from_up.at[i, 0], s.at[3], r.at[3], under),
            remote(term.at[i, near_up, 0], from_down.at[i, 0], s.at[4], r.at[4], over),
            remote(term.at[i, near_down, 1], from_up.at[i, 1], s.at[5], r.at[5], under),
        ]

    def relay(i):
        copies = coil_copies(i)
        copies[0].wait_recv()
        term[i, near_up, 0] = term[i, near_up, 0] + via_up[i]
        copies[4].start()
        copies[1].wait_recv()
        term[i, near_down, 1] = term[i, near_down, 1] + via_down[i]
        copies[5].start()

    def plane_back(i, carry):
        remote(outgoing.at[i], plane.at[i, core], pair_send.at[i], pair_recv.at[i], sibling).wait_recv()
        near_half, far_half = plane[i, :, pl.ds(0, 8)], plane[i, :, pl.ds(8, 8)]
        even = dot(left[0], tall((near_half + far_half).reshape(N, N)))
        odd = dot(left[1], tall((near_half - far_half).reshape(N, N)))
        halves_z = []
        for k in range(2):
            lanes = slice(k * TILE, (k + 1) * TILE)
            stacked = jnp.concatenate(
                [jnp.concatenate([v[:TILE, lanes], v[TILE:, lanes]], 1) for v in (even, odd)], 0
            )
            halves_z.append(dot(wide(stacked), right[k]))
        first, second = halves_z[0] + halves_z[1], halves_z[0] - halves_z[1]
        for copy in halved(sens.at[0], sens_buf, sens_sem, i, 0):
            copy.wait()
        for odd in range(2):
            rows = slice(odd * TILE, (odd + 1) * TILE)
            every = pl.ds(odd, TILE, stride=2)
            here = pl.ds(32 * odd, 32)
            for half, values in enumerate((first, second)):
                lanes = pl.ds(half * TILE, TILE)
                field_re, field_im = values[rows, :TILE], values[rows, TILE:]
                sens_re, sens_im = sens_buf[0, i, half, every, :], sens_buf[1, i, half, every, :]
                term[i, :, 0, here, lanes] = (sens_re * field_re + sens_im * field_im).reshape(RING, 32, TILE)
                term[i, :, 1, here, lanes] = (sens_re * field_im - sens_im * field_re).reshape(RING, 32, TILE)
        for copy in coil_copies(i)[:4]:
            copy.start()

        @pl.when(i > 0)
        def _():
            relay(i - 1)

        return carry

    lax.fori_loop(0, PLANES, plane_back, 0)
    relay(PLANES - 1)

    def halved_out(i):
        return [
            pltpu.make_async_copy(result.at[:, i, half], out.at[:, i, :, pl.ds(half * TILE, TILE)], sens_sem.at[i, half])
            for half in range(2)
        ]

    def collect(i, carry):
        copies = coil_copies(i)
        for k in (2, 3, 4, 5):
            copies[k].wait_recv()
        total = term[i, coil] + from_down[i] + from_up[i]
        for part in range(2):
            for odd in range(2):
                for half in range(2):
                    values = total[part, 32 * odd : 32 * odd + 32, half * TILE : (half + 1) * TILE]
                    result[part, i, half, pl.ds(odd, 32, stride=2), :] = values
        for copy in halved_out(i):
            copy.start()
        for copy in copies:
            copy.wait_send()
        return carry

    def stored(i, carry):
        for copy in halved_out(i):
            copy.wait()
        return carry

    lax.fori_loop(0, PLANES, collect, 0)
    lax.fori_loop(0, PLANES, stored, 0)
    for ring in (a1, b1, a2, b2):
        ring.drain()
    for copy in pair:
        copy.wait_send()


def gather(back, bins_row, bins_col, sens, tab):
    quarter = N // RING
    vmem = pl.BlockSpec(memory_space=pltpu.VMEM)
    hbm = pl.BlockSpec(memory_space=pl.ANY)
    return pl.pallas_call(
        gather_kernel,
        out_shape=jax.ShapeDtypeStruct((2, PLANES, quarter, N), F32),
        in_specs=[vmem, vmem, vmem, hbm, vmem, vmem, hbm],
        out_specs=hbm,
        scratch_shapes=[
            pltpu.VMEM((RING, RING * SLOTS, TILE), F32),
            pltpu.VMEM((RING, RING * SLOTS, TILE), F32),
            pltpu.VMEM((RING, SLOTS, TILE), F32),
            pltpu.VMEM((RING, SLOTS, TILE), F32),
            pltpu.VMEM((4 * TILE, N), BF16),
            pltpu.VMEM((2, PLANES, 2, N, TILE), F32),
            pltpu.VMEM((PLANES, 2, CHIPS, 2, 8, N), F32),
            pltpu.VMEM((PLANES, CHIPS, 2, 8, N), F32),
            pltpu.VMEM((PLANES, RING, 2, quarter, N), F32),
            pltpu.VMEM((PLANES, quarter, N), F32),
            pltpu.VMEM((PLANES, quarter, N), F32),
            pltpu.VMEM((PLANES, 2, quarter, N), F32),
            pltpu.VMEM((PLANES, 2, quarter, N), F32),
            pltpu.VMEM((2, PLANES, 2, quarter, TILE), F32),
            pltpu.SemaphoreType.DMA((1,)),
            pltpu.SemaphoreType.DMA((PLANES, 2)),
            pltpu.SemaphoreType.DMA((4, 4)),
            pltpu.SemaphoreType.DMA((4, 4)),
            pltpu.SemaphoreType.DMA((PLANES,)),
            pltpu.SemaphoreType.DMA((PLANES,)),
            pltpu.SemaphoreType.DMA((PLANES, 6)),
            pltpu.SemaphoreType.DMA((PLANES, 6)),
        ],
        compiler_params=pltpu.CompilerParams(collective_id=1, has_side_effects=True, vmem_limit_bytes=VMEM_LIMIT),
    )(back, bins_row, bins_col, tab["phases_t"], tab["back_left"], tab["back_right"], sens)


def body(image, sens, weights, bins, counts):
    tab = {name: jnp.asarray(table) for name, table in tables().items()}
    tiles, bins_row, bins_col, side = scatter(image, sens, bins.reshape(1, SLOTS), tab)
    back = grid(counts, tiles, side, weights, tab)
    return gather(back, bins_row, bins_col, sens, tab)


def solution(mesh):
    in_specs = (
        P(None, "slab", None, None),
        P("coil", None, "slab", None, None),
        P("slab", None, None),
        P("slab"),
        P("slab"),
    )
    out_specs = P(None, "slab", "coil", None)
    return jax.shard_map(body, mesh=mesh, in_specs=in_specs, out_specs=out_specs, check_vma=False)
```

```python
import functools

import numpy as np
import jax
import jax.numpy as jnp
import ml_dtypes
from jax import lax
from jax.experimental import pallas as pl
from jax.experimental.pallas import tpu as pltpu
from jax.sharding import PartitionSpec as P

N = 256
TILE = 128
SLOTS = 256
CHIPS = 16
RING = 4
PLANES = 8
GROUPS = 2
SPAN = SLOTS // GROUPS
VMEM_LIMIT = 60 * 1024 * 1024
F32 = jnp.float32
BF16 = jnp.bfloat16


def halves(values):
    high = values.astype(ml_dtypes.bfloat16)
    low = (values - high.astype(np.float64)).astype(ml_dtypes.bfloat16)
    return high, low


def stack(table, axis):
    high, low = halves(table)
    return np.concatenate([high, low, high], axis)


def wave(rows, columns):
    angle = 2.0 * np.pi * (rows[:, None] * columns[None, :] % N) / N
    return np.cos(angle) / 16.0, np.sin(angle) / 16.0


EVEN = 2 * np.arange(TILE)
ODD = (2 * np.arange(TILE) + 1 + TILE) % N


def tables():
    first = np.arange(TILE)
    fwd_right, fwd_left, back_left, back_right = [], [], [], []
    packed = np.arange(2 * TILE).reshape(2, PLANES, 2, 8).transpose(2, 1, 0, 3).reshape(-1)
    for odd in range(2):
        cosine, sine = wave(first, (EVEN, ODD)[odd])
        fwd_right.append(stack(np.block([[cosine, -sine], [sine, cosine]]), 0))
        cosine, sine = wave((EVEN, ODD)[odd], first)
        back_right.append(stack(np.block([[cosine, sine], [-sine, cosine]]), 0))
        cosine, sine = wave(first, 2 * first + odd)
        fwd_left.append(stack(np.block([[cosine, sine], [-sine, cosine]]), 1))
        cosine, sine = wave(2 * first + odd, first)
        back_left.append(stack(np.block([[cosine, -sine], [sine, cosine]])[:, packed], 1))
    lanes = []
    cosine, sine = wave(np.arange(N), np.arange(N))
    for chip in range(CHIPS):
        cos_x = np.repeat(cosine[:, chip * 16 : chip * 16 + 16], 8, axis=1)
        sin_x = np.repeat(sine[:, chip * 16 : chip * 16 + 16], 8, axis=1)
        cos_parts, sin_parts = halves(cos_x), halves(sin_x)
        lanes.append(np.concatenate([cos_parts[0], sin_parts[0], cos_parts[1], sin_parts[1]], 1))
    phases = np.stack(lanes)
    lane = np.arange(TILE)
    order = np.stack([np.where(lane < 64, 2 * lane, 2 * lane - TILE + 1), np.where(lane < 64, 2 * lane + 1, 2 * lane - TILE)])
    natural = np.concatenate([np.eye(TILE)[order[0]], np.eye(TILE)[order[1]]], 0).astype(ml_dtypes.bfloat16)
    return {
        "fwd_right": np.stack(fwd_right),
        "fwd_left": np.stack(fwd_left),
        "back_left": np.stack(back_left),
        "back_right": np.stack(back_right),
        "phases": phases,
        "phases_t": np.ascontiguousarray(phases.transpose(0, 2, 1)),
        "natural": natural,
        "packed": np.ascontiguousarray(natural.T),
    }


def split(values):
    high = values.astype(BF16)
    low = (values - high.astype(F32)).astype(BF16)
    return high, low


def dot(a, b):
    return lax.dot_general(a, b, (((1,), (0,)), ((), ())), preferred_element_type=F32)


def wide(values):
    high, low = split(values)
    return jnp.concatenate([high, high, low], 1)


def tall(values):
    high, low = split(values)
    return jnp.concatenate([high, high, low], 0)


def place():
    slab = lax.axis_index("slab")
    core = lax.rem(slab, 2)
    chip = slab // 2
    x, y = lax.rem(chip, RING), chip // RING
    return core, chip, x, y


def device(x, y, core):
    return {"slab": (y * RING + x) * 2 + core}


def up(i, step=1):
    return lax.rem(i + step, RING)


def down(i):
    return lax.rem(i + RING - 1, RING)


def halved(source, target, sem, i, first):
    return [
        pltpu.make_async_copy(source.at[:, i, :, pl.ds(half * TILE, TILE)], target.at[:, i, half], sem.at[i, first + half])
        for half in range(2)
    ]


def greet(peers):
    barrier = pltpu.get_barrier_semaphore()
    for peer in peers:
        pl.semaphore_signal(barrier, inc=1, device_id=peer, device_id_type=pl.DeviceIdType.MESH)


def remote(src, dst, send, recv, peer):
    return pltpu.make_async_remote_copy(
        src_ref=src, dst_ref=dst, send_sem=send, recv_sem=recv, device_id=peer, device_id_type=pl.DeviceIdType.MESH
    )


class RingSum:
    def __init__(self, src, via_up, via_down, from_down, from_up, send, recv, me, above, below):
        self.src, self.me = src, me
        rows = src.shape[1]
        self.half = (pl.ds(0, rows // 2), pl.ds(rows // 2, rows // 2))
        self.via_up, self.via_down, self.from_down, self.from_up = via_up, via_down, from_down, from_up
        first, second = self.half
        far, near_up, near_down = up(me, 2), up(me), down(me)
        self.copies = [
            remote(src.at[far, first], via_up, send.at[0], recv.at[0], above),
            remote(src.at[far, second], via_down, send.at[1], recv.at[1], below),
            remote(src.at[near_up, second], from_down.at[second], send.at[2], recv.at[2], above),
            remote(src.at[near_down, first], from_up.at[first], send.at[3], recv.at[3], below),
            remote(src.at[near_up, first], from_down.at[first], send.at[4], recv.at[4], above),
            remote(src.at[near_down, second], from_up.at[second], send.at[5], recv.at[5], below),
        ]

    def far(self):
        for copy in self.copies[:2]:
            copy.start()

    def near(self):
        for copy in self.copies[2:4]:
            copy.start()

    def relay(self):
        first, second = self.half
        self.copies[0].wait_recv()
        near = up(self.me)
        self.src[near, first] = self.src[near, first] + self.via_up[...]
        self.copies[4].start()
        self.copies[1].wait_recv()
        near = down(self.me)
        self.src[near, second] = self.src[near, second] + self.via_down[...]
        self.copies[5].start()

    def arrive(self):
        for k in (2, 3, 4, 5):
            self.copies[k].wait_recv()

    def total(self, rows):
        return self.src[self.me, rows] + self.from_down[rows] + self.from_up[rows]

    def drain(self):
        for copy in self.copies:
            copy.wait_send()


class PlaneGather:
    def __init__(self, buf, send, recv, outer, inner, outer_up, outer_down, inner_up, inner_down):
        rows = buf.shape[2]
        first, second = pl.ds(0, rows // 2), pl.ds(rows // 2, rows // 2)
        row, below, above = buf.at[outer], buf.at[down(outer)], buf.at[up(outer)]

        def same(ref, k, peer):
            return remote(ref, ref, send.at[k], recv.at[k], peer)

        self.inner = [
            same(row.at[inner], 0, inner_up),
            same(row.at[inner], 1, inner_down),
            same(row.at[down(inner), first], 2, inner_up),
            same(row.at[up(inner), second], 3, inner_down),
        ]
        pieces = [inner, down(inner), up(inner), up(inner, 2)]
        self.direct = [(same(row.at[p], 4 + 2 * k, outer_up), same(row.at[p], 5 + 2 * k, outer_down)) for k, p in enumerate(pieces)]
        self.relays = [
            (same(below.at[p, first], 12 + 2 * k, outer_up), same(above.at[p, second], 13 + 2 * k, outer_down))
            for k, p in enumerate(pieces)
        ]

    def begin(self):
        for copy in self.inner[:2] + list(self.direct[0]):
            copy.start()

    def pass_inner(self):
        for k in range(2):
            self.inner[k].wait_recv()
            self.inner[2 + k].start()
            for copy in self.direct[1 + k]:
                copy.start()

    def last_inner(self):
        for k in (2, 3):
            self.inner[k].wait_recv()
        for copy in self.direct[3]:
            copy.start()

    def relay(self, piece):
        for k in range(2):
            self.direct[piece][k].wait_recv()
            self.relays[piece][k].start()

    def last(self):
        for pair in self.relays:
            for copy in pair:
                copy.wait_recv()

    def drain(self):
        for copy in self.inner + [copy for pair in self.direct + self.relays for copy in pair]:
            copy.wait_send()


def kernel(
    image, sens, bins, live, weights, fwd_right, fwd_left, back_left, back_right, natural, packed, phases, phases_t, out,
    image_buf, sens_buf, weight_buf, field, table, table_t, bins_row, bins_col, sums_a, sums_b, mids,
    via_up1, via_down1, from_down1, from_up1, via_up2, via_down2, from_down2, from_up2,
    mixed, gridded, all_a, all_b, planes_back, via_up, via_down, from_down, from_up, result,
    load_sem, weight_sem, table_sem, out_sem, bin_send, bin_recv, pair_send, pair_recv, ring_send, ring_recv,
    all_send, all_recv, slab_send, slab_recv, coil_send, coil_recv,
):
    core, chip, x, y = place()
    coil = lax.axis_index("coil")
    sibling = device(x, y, 1 - core)
    east, west = device(up(x), y, core), device(down(x), y, core)
    north, south = device(x, up(y), core), device(x, down(y), core)
    over, under = {"coil": up(coil)}, {"coil": down(coil)}
    others = [{"slab": lax.rem(chip + k, CHIPS) * 2 + core} for k in range(1, CHIPS)]
    peers = [sibling, over, under] + others
    greet(peers)

    def loads(i):
        return halved(image, image_buf, load_sem, i, 0) + halved(sens.at[0], sens_buf, load_sem, i, 2)

    def start_load(i, carry):
        for copy in loads(i):
            copy.start()
        return carry

    lax.fori_loop(0, PLANES, start_load, 0)
    fetch = pltpu.make_async_copy(phases.at[chip], table, table_sem.at[0])
    fetch_t = pltpu.make_async_copy(phases_t.at[chip], table_t, table_sem.at[1])
    fetch_weights = pltpu.make_async_copy(weights, weight_buf, weight_sem)
    fetch.start()
    bins_row[chip] = jnp.broadcast_to(bins[...].astype(F32), (8, SLOTS))
    spread = [remote(bins_row.at[chip], bins_row.at[chip], bin_send.at[k], bin_recv.at[k], others[k]) for k in range(CHIPS - 1)]

    def pair(i):
        return remote(field.at[2, i], field.at[core, i], pair_send.at[i], pair_recv.at[i], sibling)

    def plane_forward(i):
        for copy in loads(i):
            copy.wait()
        summed, differed = [], []
        for odd in range(2):
            rows = pl.ds(odd, TILE, stride=2)
            parts = []
            for half in range(2):
                image_re, image_im = image_buf[0, i, half, rows, :], image_buf[1, i, half, rows, :]
                sens_re, sens_im = sens_buf[0, i, half, rows, :], sens_buf[1, i, half, rows, :]
                parts.append((sens_re * image_re - sens_im * image_im, sens_re * image_im + sens_im * image_re))
            summed.append(jnp.concatenate([parts[0][k] + parts[1][k] for k in range(2)], 1))
            differed.append(jnp.concatenate([parts[0][k] - parts[1][k] for k in range(2)], 1))
        even_z = dot(wide(jnp.concatenate(summed, 0)), fwd_right[0])
        odd_z = dot(wide(jnp.concatenate(differed, 0)), fwd_right[1])
        parts = []
        for odd in range(2):
            rows = slice(odd * TILE, (odd + 1) * TILE)
            stacked = jnp.concatenate(
                [
                    jnp.concatenate([even_z[rows, :TILE], odd_z[rows, :TILE]], 1),
                    jnp.concatenate([even_z[rows, TILE:], odd_z[rows, TILE:]], 1),
                ],
                0,
            )
            parts.append(dot(fwd_left[odd], tall(stacked)))
        for side, values in enumerate((parts[0] + parts[1], parts[0] - parts[1])):
            values = values.reshape(2, 8, 2, 8, N)
            for part in range(2):
                field[2 * core, i, pl.ds(8 * side, 8), part] = values[part, :, 0]
                field[2 - core, i, pl.ds(8 * side, 8), part] = values[part, :, 1]

    def plane_and_pair(i, carry):
        plane_forward(i)
        pair(i).start()
        return carry

    plane_forward(0)
    pl.semaphore_wait(pltpu.get_barrier_semaphore(), len(peers))
    pair(0).start()
    for copy in spread:
        copy.start()
    lax.fori_loop(1, PLANES, plane_and_pair, 0)
    fetch_weights.start()
    fetch_t.start()
    fetch.wait()
    for copy in spread:
        copy.wait_recv()
    bins_col[...] = bins_row[...].reshape(CHIPS * 8, SLOTS).T
    lane = lax.broadcasted_iota(jnp.int32, (SLOTS, TILE), 1)

    def column(p):
        return jnp.sum(jnp.where(lane == 8 * p, bins_col[...], 0.0), axis=1, keepdims=True).astype(jnp.int32)

    own_side = jnp.broadcast_to(column(chip) % 2, (SLOTS, TILE)) == 1

    def slab_sums(px, py):
        p = py * RING + px
        index = column(p)
        kx, ky, side = index // 16, (index // 2) % 8, index % 2
        hot = jnp.where(lax.broadcasted_iota(jnp.int32, (SLOTS, N), 1) == kx, 1.0, 0.0).astype(BF16)
        phase = dot(hot, table[...])
        row = lax.broadcasted_iota(jnp.int32, (SLOTS, 4 * TILE), 1) % 8
        phase = jnp.where(row == ky, phase, 0.0).astype(BF16)
        mats = []
        for k in range(2):
            cosine, sine = phase[:, 2 * k * TILE : (2 * k + 1) * TILE], phase[:, (2 * k + 1) * TILE : (2 * k + 2) * TILE]
            mats.append(jnp.concatenate([jnp.concatenate([cosine, sine], 1), jnp.concatenate([-sine, cosine], 1)], 0))
        rows = jnp.concatenate([field[c, :, p, part].reshape(64, N) for part in range(2) for c in range(2)], 0)
        sums = dot(jnp.concatenate([mats[0], mats[1], mats[0]], 1), tall(rows))
        low_lane = jnp.where(lane < 64, 0, 1) == side
        sums_re = jnp.where(low_lane, sums[:SLOTS, :TILE], sums[:SLOTS, TILE:])
        sums_im = jnp.where(low_lane, sums[SLOTS:, :TILE], sums[SLOTS:, TILE:])
        for g in range(GROUPS):
            sums_a[g, px, pl.ds(py * SPAN, SPAN)] = sums_re[g * SPAN : (g + 1) * SPAN]
            sums_b[g, py, pl.ds(px * SPAN, SPAN)] = sums_im[g * SPAN : (g + 1) * SPAN]

    def over_slabs(one):
        def far_column(k, carry):
            one(up(x, 2), up(y, k))
            return carry

        def far_row(k, carry):
            one(up(x, 3 + k), up(y, 2))
            return carry

        def near(k, carry):
            one(up(x, 3 + k % 3), up(y, 3 + k // 3))
            return carry

        def far():
            lax.fori_loop(0, 4, far_column, 0, unroll=2)
            lax.fori_loop(0, 3, far_row, 0, unroll=3)

        return far, lambda start, stop, unroll: lax.fori_loop(start, stop, near, 0, unroll=unroll)

    first, second = [], []
    for g in range(GROUPS):
        for half in range(2):
            k = 2 * g + half
            ring = (x, east, west) if half == 0 else (y, north, south)
            src = (sums_a, sums_b)[half].at[g]
            first.append(RingSum(src, via_up1.at[k], via_down1.at[k], from_down1.at[k], from_up1.at[k], ring_send.at[k], ring_recv.at[k], *ring))
            ring = (y, north, south) if half == 0 else (x, east, west)
            j = 2 * GROUPS + k
            second.append(RingSum(mids.at[k], via_up2.at[k], via_down2.at[k], from_down2.at[k], from_up2.at[k], ring_send.at[j], ring_recv.at[j], *ring))
    gathers = []
    for g in range(GROUPS):
        gathers.append(
            (
                PlaneGather(all_a.at[g], all_send.at[2 * g], all_recv.at[2 * g], x, y, east, west, north, south),
                PlaneGather(all_b.at[g], all_send.at[2 * g + 1], all_recv.at[2 * g + 1], y, x, north, south, east, west),
            )
        )

    def rings(which, g, action):
        for ring in which[2 * g : 2 * g + 2]:
            getattr(ring, action)()

    def middle(g):
        for k in (2 * g, 2 * g + 1):
            first[k].arrive()
            for m in range(RING):
                mids[k, m] = first[k].total(pl.ds(m * SPAN, SPAN))
            second[k].far()
            second[k].near()

    def grid(g):
        rings(second, g, "arrive")
        values = jnp.concatenate([second[2 * g].total(pl.ds(0, SPAN)), second[2 * g + 1].total(pl.ds(0, SPAN))], 0)
        upper = own_side[g * SPAN : (g + 1) * SPAN]
        upper = jnp.concatenate([upper] * 4, 0)
        high = values.astype(BF16).astype(F32)
        both = jnp.concatenate([high, values - high], 0)
        both = jnp.concatenate([jnp.where(upper, 0.0, both), jnp.where(upper, both, 0.0)], 1).astype(BF16)
        mixed[...] = dot(both, natural[...]).reshape(4, SPAN, TILE)

        def unit(k, carry):
            row = lax.broadcasted_iota(jnp.int32, (32, TILE), 0) % 8
            rows = [pl.ds(16 * k + 8 * u, 8) for u in range(2)]
            low = [mixed[:, r].reshape(32, TILE).astype(BF16) for r in rows]
            none = jnp.zeros((32, TILE), BF16)
            lhs = jnp.concatenate([jnp.concatenate([low[0], none], 1), jnp.concatenate([none, low[1]], 1)], 0)
            mat = jnp.concatenate([weight_buf[pl.ds(g * SPAN + 16 * k + 8 * u, 8)].reshape(8 * TILE, TILE) for u in range(2)], 1)
            spread = lax.dot_general(lhs, mat, (((1,), (1,)), ((), ())), preferred_element_type=F32)
            masked = []
            for u in range(2):
                samples = jnp.zeros((32, TILE), F32)
                for j in range(8):
                    samples = jnp.where(row == j, spread[32 * u : 32 * u + 32, j * TILE : (j + 1) * TILE], samples)
                samples = samples[:16] + samples[16:]
                high = samples.astype(BF16).astype(F32)
                both = jnp.concatenate([high, samples - high], 0)
                masked.append(jnp.concatenate([jnp.where(row == j, both, 0.0).astype(BF16) for j in range(8)], 1))
            back = dot(jnp.concatenate(masked, 0), mat)
            for u in range(2):
                values = back[32 * u : 32 * u + 32, u * TILE : (u + 1) * TILE]
                values = values[:16] + values[16:]
                gridded[0, rows[u]] = values[:8]
                gridded[1, rows[u]] = values[8:]
            return carry

        lax.fori_loop(0, SPAN // 16, unit, 0, unroll=4)
        high, low = split(gridded[...].reshape(2 * SPAN, TILE))
        back = dot(jnp.concatenate([high, low], 0), packed[...])
        back = jnp.where(upper, back[:, TILE:], back[:, :TILE])
        back = back[: 2 * SPAN] + back[2 * SPAN :]
        slot = g * SPAN + lax.broadcasted_iota(jnp.int32, (2 * SPAN, TILE), 0) % SPAN
        back = jnp.where(slot < live[0], back, 0.0)
        all_a[g, x, y] = back[:SPAN]
        all_b[g, y, x] = back[SPAN:]

    def slab_pair(p):
        return remote(planes_back.at[2, p], planes_back.at[core, p], slab_send.at[p], slab_recv.at[p], sibling)

    def slab_back(g, px, py):
        p = py * RING + px
        side = column(p)[g * SPAN : (g + 1) * SPAN] % 2
        index = bins_row[p, 0:1, pl.ds(g * SPAN, SPAN)].astype(jnp.int32)
        kx, ky = index // 16, (index // 2) % 8
        hot = jnp.where(lax.broadcasted_iota(jnp.int32, (N, SPAN), 0) == kx, 1.0, 0.0).astype(BF16)
        phase = dot(table_t[...], hot)
        row = lax.broadcasted_iota(jnp.int32, (4 * TILE, SPAN), 0) % 8
        phase = jnp.where(row == ky, phase, 0.0).astype(BF16)
        mats = []
        for k in range(2):
            cosine, sine = phase[2 * k * TILE : (2 * k + 1) * TILE], phase[(2 * k + 1) * TILE : (2 * k + 2) * TILE]
            mats.append(jnp.concatenate([jnp.concatenate([cosine, -sine], 1), jnp.concatenate([sine, cosine], 1)], 0))
        tiles = jnp.concatenate([all_a[g, px, py], all_b[g, py, px]], 0)
        low_lane = jnp.where(lane[:SPAN] < 64, 0, 1) == side
        low_lane = jnp.concatenate([low_lane, low_lane], 0)
        tiles = jnp.concatenate([jnp.where(low_lane, tiles, 0.0), jnp.where(low_lane, 0.0, tiles)], 1)
        sums = dot(jnp.concatenate([mats[0], mats[1], mats[0]], 1), tall(tiles))
        sums = sums.reshape(2, 2, PLANES, 8, N)
        for part in range(2):
            for source, slot in ((0, 2 * core), (1, 2 - core)):
                values = sums[part, source]
                if g > 0:
                    values = values + planes_back[slot, p, :, part]
                planes_back[slot, p, :, part] = values
        if g == GROUPS - 1:
            slab_pair(p).start()

    far_sums, near_sums = over_slabs(slab_sums)

    def arrived(i, carry):
        pair(i).wait_recv()
        return carry

    lax.fori_loop(0, PLANES, arrived, 0)
    far_sums()
    rings(first, 0, "far")
    near_sums(0, 4, 2)
    near_sums(5, 9, 2)
    rings(first, 0, "near")
    slab_sums(x, y)
    rings(first, 0, "relay")
    if GROUPS == 2:
        rings(first, 1, "far")
    middle(0)
    if GROUPS == 2:
        rings(first, 1, "near")
        rings(first, 1, "relay")
    rings(second, 0, "relay")
    fetch_weights.wait()
    fetch_t.wait()
    grid(0)

    def both(g, action, *args):
        for gather in gathers[g]:
            getattr(gather, action)(*args)

    both(0, "begin")
    if GROUPS == 2:
        middle(1)
        both(0, "pass_inner")
        rings(second, 1, "relay")
        both(0, "relay", 0)
        grid(1)
        both(1, "begin")
    else:
        both(0, "pass_inner")
        both(0, "relay", 0)
    both(0, "last_inner")
    both(0, "relay", 1)
    both(0, "relay", 2)
    if GROUPS == 2:
        both(1, "pass_inner")
    both(0, "relay", 3)
    for g in range(GROUPS):
        far_back, near_back = over_slabs(functools.partial(slab_back, g))
        if g == 1:
            both(1, "last_inner")
            both(1, "relay", 1)
            both(1, "relay", 2)
            both(1, "relay", 3)
        near_back(0, 9, 3)
        if g == 0 and GROUPS == 2:
            both(1, "relay", 0)
        both(g, "last")
        far_back()

    def slabs_arrived(p, carry):
        slab_pair(p).wait_recv()
        return carry

    lax.fori_loop(0, CHIPS, slabs_arrived, 0)

    term = image_buf
    quarter = N // RING
    far, near_up, near_down = up(coil, 2), up(coil), down(coil)

    def share(part, i, q):
        return term.at[part, i, :, pl.ds(pl.multiple_of(q * quarter, quarter), quarter)]

    def coil_copy(i, k):
        source, target, peer = (
            (share(0, i, far), via_up.at[i], over),
            (share(1, i, far), via_down.at[i], under),
            (share(1, i, near_up), from_down.at[i, 1], over),
            (share(0, i, near_down), from_up.at[i, 0], under),
            (share(0, i, near_up), from_down.at[i, 0], over),
            (share(1, i, near_down), from_up.at[i, 1], under),
        )[k]
        return remote(source, target, coil_send.at[i, k], coil_recv.at[i, k], peer)

    def coil_relay(i):
        coil_copy(i, 0).wait_recv()
        ref = share(0, i, near_up)
        ref[...] = ref[...] + via_up[i]
        coil_copy(i, 4).start()
        coil_copy(i, 1).wait_recv()
        ref = share(1, i, near_down)
        ref[...] = ref[...] + via_down[i]
        coil_copy(i, 5).start()

    def plane_back(i, carry):
        near_half, far_half = planes_back[pl.ds(0, 2), pl.ds(0, 8), i], planes_back[pl.ds(0, 2), pl.ds(8, 8), i]
        even = dot(back_left[0], tall((near_half + far_half).reshape(N, N)))
        odd = dot(back_left[1], tall((near_half - far_half).reshape(N, N)))
        halves_z = []
        for k in range(2):
            lanes = slice(k * TILE, (k + 1) * TILE)
            stacked = jnp.concatenate([jnp.concatenate([v[:TILE, lanes], v[TILE:, lanes]], 1) for v in (even, odd)], 0)
            halves_z.append(dot(wide(stacked), back_right[k]))
        for half, values in enumerate((halves_z[0] + halves_z[1], halves_z[0] - halves_z[1])):
            for odd in range(2):
                rows = slice(odd * TILE, (odd + 1) * TILE)
                field_re, field_im = values[rows, :TILE], values[rows, TILE:]
                every = pl.ds(odd, TILE, stride=2)
                sens_re, sens_im = sens_buf[0, i, half, every, :], sens_buf[1, i, half, every, :]
                term[0, i, half, every, :] = sens_re * field_re + sens_im * field_im
                term[1, i, half, every, :] = sens_re * field_im - sens_im * field_re
        for k in range(4):
            coil_copy(i, k).start()

        @pl.when(i > 0)
        def _():
            coil_relay(i - 1)

        return carry

    lax.fori_loop(0, PLANES, plane_back, 0)
    coil_relay(PLANES - 1)

    def store(i):
        return pltpu.make_async_copy(result.at[:, i], out.at[:, i], out_sem.at[i])

    def collect(i, carry):
        for k in (2, 3, 4, 5):
            coil_copy(i, k).wait_recv()
        for part in range(2):
            total = share(part, i, coil)[...] + from_down[i, part] + from_up[i, part]
            for half in range(2):
                result[part, i, :, half * TILE : (half + 1) * TILE] = total[half]
        store(i).start()
        for k in range(6):
            coil_copy(i, k).wait_send()
        return carry

    def finished(i, carry):
        store(i).wait()
        pair(i).wait_send()
        return carry

    def slabs_sent(p, carry):
        slab_pair(p).wait_send()
        return carry

    lax.fori_loop(0, PLANES, collect, 0)
    lax.fori_loop(0, PLANES, finished, 0)
    lax.fori_loop(0, CHIPS, slabs_sent, 0)
    for ring in first + second:
        ring.drain()
    for g in range(GROUPS):
        both(g, "drain")
    for copy in spread:
        copy.wait_send()


def fused(image, sens, bins, live, weights, tab):
    quarter = N // RING
    rings = 2 * GROUPS
    vmem = pl.BlockSpec(memory_space=pltpu.VMEM)
    hbm = pl.BlockSpec(memory_space=pl.ANY)
    smem = pl.BlockSpec(memory_space=pltpu.SMEM)
    return pl.pallas_call(
        kernel,
        out_shape=jax.ShapeDtypeStruct((2, PLANES, quarter, N), F32),
        in_specs=[hbm, hbm, vmem, smem, hbm] + [vmem] * 6 + [hbm] * 2,
        out_specs=hbm,
        scratch_shapes=[
            pltpu.VMEM((2, PLANES, 2, N, TILE), F32),
            pltpu.VMEM((2, PLANES, 2, N, TILE), F32),
            pltpu.VMEM((SLOTS, TILE, TILE), BF16),
            pltpu.VMEM((3, PLANES, CHIPS, 2, 8, N), F32),
            pltpu.VMEM((N, 4 * TILE), BF16),
            pltpu.VMEM((4 * TILE, N), BF16),
            pltpu.VMEM((CHIPS, 8, SLOTS), F32),
            pltpu.VMEM((SLOTS, CHIPS * 8), F32),
            pltpu.VMEM((GROUPS, RING, RING * SPAN, TILE), F32),
            pltpu.VMEM((GROUPS, RING, RING * SPAN, TILE), F32),
            pltpu.VMEM((rings, RING, SPAN, TILE), F32),
            pltpu.VMEM((rings, 2 * SPAN, TILE), F32),
            pltpu.VMEM((rings, 2 * SPAN, TILE), F32),
            pltpu.VMEM((rings, 4 * SPAN, TILE), F32),
            pltpu.VMEM((rings, 4 * SPAN, TILE), F32),
            pltpu.VMEM((rings, SPAN // 2, TILE), F32),
            pltpu.VMEM((rings, SPAN // 2, TILE), F32),
            pltpu.VMEM((rings, SPAN, TILE), F32),
            pltpu.VMEM((rings, SPAN, TILE), F32),
            pltpu.VMEM((4, SPAN, TILE), F32),
            pltpu.VMEM((2, SPAN, TILE), F32),
            pltpu.VMEM((GROUPS, RING, RING, SPAN, TILE), F32),
            pltpu.VMEM((GROUPS, RING, RING, SPAN, TILE), F32),
            pltpu.VMEM((3, CHIPS, PLANES, 2, 8, N), F32),
            pltpu.VMEM((PLANES, 2, quarter, TILE), F32),
            pltpu.VMEM((PLANES, 2, quarter, TILE), F32),
            pltpu.VMEM((PLANES, 2, 2, quarter, TILE), F32),
            pltpu.VMEM((PLANES, 2, 2, quarter, TILE), F32),
            pltpu.VMEM((2, PLANES, quarter, N), F32),
            pltpu.SemaphoreType.DMA((PLANES, 4)),
            pltpu.SemaphoreType.DMA,
            pltpu.SemaphoreType.DMA((2,)),
            pltpu.SemaphoreType.DMA((PLANES,)),
            pltpu.SemaphoreType.DMA((CHIPS - 1,)),
            pltpu.SemaphoreType.DMA((CHIPS - 1,)),
            pltpu.SemaphoreType.DMA((PLANES,)),
            pltpu.SemaphoreType.DMA((PLANES,)),
            pltpu.SemaphoreType.DMA((2 * rings, 6)),
            pltpu.SemaphoreType.DMA((2 * rings, 6)),
            pltpu.SemaphoreType.DMA((rings, 20)),
            pltpu.SemaphoreType.DMA((rings, 20)),
            pltpu.SemaphoreType.DMA((CHIPS,)),
            pltpu.SemaphoreType.DMA((CHIPS,)),
            pltpu.SemaphoreType.DMA((PLANES, 6)),
            pltpu.SemaphoreType.DMA((PLANES, 6)),
        ],
        compiler_params=pltpu.CompilerParams(collective_id=0, has_side_effects=True, vmem_limit_bytes=VMEM_LIMIT),
    )(
        image, sens, bins, live, weights, tab["fwd_right"], tab["fwd_left"], tab["back_left"], tab["back_right"],
        tab["natural"], tab["packed"], tab["phases"], tab["phases_t"],
    )


def body(image, sens, weights, bins, counts):
    tab = {name: jnp.asarray(table) for name, table in tables().items()}
    return fused(image, sens, bins.reshape(1, SLOTS), counts, weights, tab)


def solution(mesh):
    in_specs = (
        P(None, "slab", None, None),
        P("coil", None, "slab", None, None),
        P("slab", None, None),
        P("slab"),
        P("slab"),
    )
    out_specs = P(None, "slab", "coil", None)
    return jax.shard_map(body, mesh=mesh, in_specs=in_specs, out_specs=out_specs, check_vma=False)
```

```python
import functools

import numpy as np
import jax
import jax.numpy as jnp
import ml_dtypes
from jax import lax
from jax.experimental import pallas as pl
from jax.experimental.pallas import tpu as pltpu
from jax.sharding import PartitionSpec as P

N = 256
TILE = 128
SLOTS = 256
CHIPS = 16
RING = 4
PLANES = 8
GROUPS = 2
SPAN = SLOTS // GROUPS
VMEM_LIMIT = 60 * 1024 * 1024
F32 = jnp.float32
BF16 = jnp.bfloat16


def halves(values):
    high = values.astype(ml_dtypes.bfloat16)
    low = (values - high.astype(np.float64)).astype(ml_dtypes.bfloat16)
    return high, low


def stack(table, axis):
    high, low = halves(table)
    return np.concatenate([high, low, high], axis)


def wave(rows, columns):
    angle = 2.0 * np.pi * (rows[:, None] * columns[None, :] % N) / N
    return np.cos(angle) / 16.0, np.sin(angle) / 16.0


EVEN = 2 * np.arange(TILE)
ODD = (2 * np.arange(TILE) + 1 + TILE) % N


def tables():
    first = np.arange(TILE)
    fwd_right, fwd_left, back_left, back_right = [], [], [], []
    packed = np.arange(2 * TILE).reshape(2, PLANES, 2, 8).transpose(2, 1, 0, 3).reshape(-1)
    for odd in range(2):
        cosine, sine = wave(first, (EVEN, ODD)[odd])
        fwd_right.append(stack(np.block([[cosine, -sine], [sine, cosine]]), 0))
        cosine, sine = wave((EVEN, ODD)[odd], first)
        back_right.append(stack(np.block([[cosine, sine], [-sine, cosine]]), 0))
        cosine, sine = wave(first, 2 * first + odd)
        fwd_left.append(stack(np.block([[cosine, sine], [-sine, cosine]]), 1))
        cosine, sine = wave(2 * first + odd, first)
        back_left.append(stack(np.block([[cosine, -sine], [sine, cosine]])[:, packed], 1))
    lanes = []
    cosine, sine = wave(np.arange(N), np.arange(N))
    for chip in range(CHIPS):
        cos_x = np.repeat(cosine[:, chip * 16 : chip * 16 + 16], 8, axis=1)
        sin_x = np.repeat(sine[:, chip * 16 : chip * 16 + 16], 8, axis=1)
        cos_parts, sin_parts = halves(cos_x), halves(sin_x)
        lanes.append(np.concatenate([cos_parts[0], sin_parts[0], cos_parts[1], sin_parts[1]], 1))
    phases = np.stack(lanes)
    lane = np.arange(TILE)
    order = np.stack([np.where(lane < 64, 2 * lane, 2 * lane - TILE + 1), np.where(lane < 64, 2 * lane + 1, 2 * lane - TILE)])
    natural = np.concatenate([np.eye(TILE)[order[0]], np.eye(TILE)[order[1]]], 0).astype(ml_dtypes.bfloat16)
    return {
        "fwd_right": np.stack(fwd_right),
        "fwd_left": np.stack(fwd_left),
        "back_left": np.stack(back_left),
        "back_right": np.stack(back_right),
        "phases": phases,
        "phases_t": np.ascontiguousarray(phases.transpose(0, 2, 1)),
        "natural": natural,
        "packed": np.ascontiguousarray(natural.T),
    }


def split(values):
    high = values.astype(BF16)
    low = (values - high.astype(F32)).astype(BF16)
    return high, low


def dot(a, b):
    return lax.dot_general(a, b, (((1,), (0,)), ((), ())), preferred_element_type=F32)


def wide(values):
    high, low = split(values)
    return jnp.concatenate([high, high, low], 1)


def tall(values):
    high, low = split(values)
    return jnp.concatenate([high, high, low], 0)


def place():
    slab = lax.axis_index("slab")
    core = lax.rem(slab, 2)
    chip = slab // 2
    x, y = lax.rem(chip, RING), chip // RING
    return core, chip, x, y


def device(x, y, core):
    return {"slab": (y * RING + x) * 2 + core}


def up(i, step=1):
    return lax.rem(i + step, RING)


def down(i):
    return lax.rem(i + RING - 1, RING)


def halved(source, target, sem, i, first):
    return [
        pltpu.make_async_copy(source.at[:, i, :, pl.ds(half * TILE, TILE)], target.at[:, i, half], sem.at[i, first + half])
        for half in range(2)
    ]


def greet(peers):
    barrier = pltpu.get_barrier_semaphore()
    for peer in peers:
        pl.semaphore_signal(barrier, inc=1, device_id=peer, device_id_type=pl.DeviceIdType.MESH)


def remote(src, dst, send, recv, peer):
    return pltpu.make_async_remote_copy(
        src_ref=src, dst_ref=dst, send_sem=send, recv_sem=recv, device_id=peer, device_id_type=pl.DeviceIdType.MESH
    )


class RingSum:
    def __init__(self, src, via_up, via_down, from_down, from_up, send, recv, me, above, below):
        self.src, self.me = src, me
        rows = src.shape[1]
        self.half = (pl.ds(0, rows // 2), pl.ds(rows // 2, rows // 2))
        self.via_up, self.via_down, self.from_down, self.from_up = via_up, via_down, from_down, from_up
        first, second = self.half
        far, near_up, near_down = up(me, 2), up(me), down(me)
        self.copies = [
            remote(src.at[far, first], via_up, send.at[0], recv.at[0], above),
            remote(src.at[far, second], via_down, send.at[1], recv.at[1], below),
            remote(src.at[near_up, second], from_down.at[second], send.at[2], recv.at[2], above),
            remote(src.at[near_down, first], from_up.at[first], send.at[3], recv.at[3], below),
            remote(src.at[near_up, first], from_down.at[first], send.at[4], recv.at[4], above),
            remote(src.at[near_down, second], from_up.at[second], send.at[5], recv.at[5], below),
        ]

    def far(self):
        for copy in self.copies[:2]:
            copy.start()

    def near(self):
        for copy in self.copies[2:4]:
            copy.start()

    def relay(self):
        first, second = self.half
        self.copies[0].wait_recv()
        near = up(self.me)
        self.src[near, first] = self.src[near, first] + self.via_up[...]
        self.copies[4].start()
        self.copies[1].wait_recv()
        near = down(self.me)
        self.src[near, second] = self.src[near, second] + self.via_down[...]
        self.copies[5].start()

    def arrive(self):
        for k in (2, 3, 4, 5):
            self.copies[k].wait_recv()

    def total(self, rows):
        return self.src[self.me, rows] + self.from_down[rows] + self.from_up[rows]

    def drain(self):
        for copy in self.copies:
            copy.wait_send()


class RingDirect:
    def __init__(self, src, slots, send, recv, me, peers):
        self.src, self.slots, self.me = src, slots, me
        self.copies = [
            remote(src.at[up(me, step)], slots.at[k], send.at[k], recv.at[k], peer)
            for k, (step, peer) in enumerate(zip((2, 1, 3), peers))
        ]

    def begin(self):
        for copy in self.copies:
            copy.start()

    def arrive(self):
        for copy in self.copies:
            copy.wait_recv()

    def total(self):
        return self.src[self.me] + self.slots[0] + self.slots[1] + self.slots[2]

    def drain(self):
        for copy in self.copies:
            copy.wait_send()


class PlaneGather:
    def __init__(self, buf, send, recv, outer, inner, outer_up, outer_down, inner_up, inner_down):
        rows = buf.shape[2]
        first, second = pl.ds(0, rows // 2), pl.ds(rows // 2, rows // 2)
        row, below, above = buf.at[outer], buf.at[down(outer)], buf.at[up(outer)]

        def same(ref, k, peer):
            return remote(ref, ref, send.at[k], recv.at[k], peer)

        self.inner = [
            same(row.at[inner], 0, inner_up),
            same(row.at[inner], 1, inner_down),
            same(row.at[down(inner), first], 2, inner_up),
            same(row.at[up(inner), second], 3, inner_down),
        ]
        pieces = [inner, down(inner), up(inner), up(inner, 2)]
        self.direct = [(same(row.at[p], 4 + 2 * k, outer_up), same(row.at[p], 5 + 2 * k, outer_down)) for k, p in enumerate(pieces)]
        self.relays = [
            (same(below.at[p, first], 12 + 2 * k, outer_up), same(above.at[p, second], 13 + 2 * k, outer_down))
            for k, p in enumerate(pieces)
        ]

    def begin(self):
        for copy in self.inner[:2] + list(self.direct[0]):
            copy.start()

    def pass_inner(self):
        for k in range(2):
            self.inner[k].wait_recv()
            self.inner[2 + k].start()
            for copy in self.direct[1 + k]:
                copy.start()

    def last_inner(self):
        for k in (2, 3):
            self.inner[k].wait_recv()
        for copy in self.direct[3]:
            copy.start()

    def relay(self, piece):
        for k in range(2):
            self.direct[piece][k].wait_recv()
            self.relays[piece][k].start()

    def last(self, piece):
        for copy in self.relays[piece]:
            copy.wait_recv()

    def drain(self):
        for copy in self.inner + [copy for pair in self.direct + self.relays for copy in pair]:
            copy.wait_send()


def kernel(
    image, sens, bins, live, weights, fwd_right_hbm, fwd_left_hbm, back_left_hbm, back_right_hbm, natural_hbm, packed_hbm, phases, phases_t, out,
    fwd_right, fwd_left, back_left, back_right, natural, packed, image_buf, sens_buf, weight_buf, field, table, table_t, bins_row, bins_col, sums_a, sums_b, mids,
    via_up1, via_down1, from_down1, from_up1, slots2,
    mixed, gridded, back_phase, all_a, all_b, planes_back, via_up, via_down, from_down, from_up, result,
    load_sem, weight_sem, table_sem, out_sem, bin_send, bin_recv, pair_send, pair_recv, ring_send, ring_recv, share_send, share_recv,
    all_send, all_recv, slab_send, slab_recv, coil_send, coil_recv,
):
    core, chip, x, y = place()
    coil = lax.axis_index("coil")
    sibling = device(x, y, 1 - core)
    east, west = device(up(x), y, core), device(down(x), y, core)
    north, south = device(x, up(y), core), device(x, down(y), core)
    over, under = {"coil": up(coil)}, {"coil": down(coil)}
    others = [{"slab": lax.rem(chip + k, CHIPS) * 2 + core} for k in range(1, CHIPS)]
    peers = [sibling, over, under] + others
    def loads(i):
        return halved(image, image_buf, load_sem, i, 0) + halved(sens.at[0], sens_buf, load_sem, i, 2)

    def start_load(i, carry):
        for copy in loads(i):
            copy.start()
        return carry

    early = [pltpu.make_async_copy(fwd_right_hbm, fwd_right, table_sem.at[2]), pltpu.make_async_copy(fwd_left_hbm, fwd_left, table_sem.at[3])]
    late = [
        pltpu.make_async_copy(source, target, table_sem.at[4 + k])
        for k, (source, target) in enumerate(
            ((back_left_hbm, back_left), (back_right_hbm, back_right), (natural_hbm, natural), (packed_hbm, packed))
        )
    ]
    fetch = pltpu.make_async_copy(phases.at[chip], table, table_sem.at[0])
    fetch_t = pltpu.make_async_copy(phases_t.at[chip], table_t, table_sem.at[1])
    fetch_weights = pltpu.make_async_copy(weights, weight_buf, weight_sem)
    start_load(0, 0)
    for copy in early:
        copy.start()
    greet(peers)
    lax.fori_loop(1, PLANES, start_load, 0)
    fetch.start()
    bins_row[chip] = jnp.broadcast_to(bins[...].astype(F32), (8, SLOTS))
    spread = [remote(bins_row.at[chip], bins_row.at[chip], bin_send.at[k], bin_recv.at[k], others[k]) for k in range(CHIPS - 1)]

    def pair(i):
        return remote(field.at[2, i], field.at[core, i], pair_send.at[i], pair_recv.at[i], sibling)

    def plane_forward(i):
        for copy in loads(i):
            copy.wait()
        summed, differed = [], []
        for odd in range(2):
            rows = pl.ds(odd, TILE, stride=2)
            parts = []
            for half in range(2):
                image_re, image_im = image_buf[0, i, half, rows, :], image_buf[1, i, half, rows, :]
                sens_re, sens_im = sens_buf[0, i, half, rows, :], sens_buf[1, i, half, rows, :]
                parts.append((sens_re * image_re - sens_im * image_im, sens_re * image_im + sens_im * image_re))
            summed.append(jnp.concatenate([parts[0][k] + parts[1][k] for k in range(2)], 1))
            differed.append(jnp.concatenate([parts[0][k] - parts[1][k] for k in range(2)], 1))
        even_z = dot(wide(jnp.concatenate(summed, 0)), fwd_right[0])
        odd_z = dot(wide(jnp.concatenate(differed, 0)), fwd_right[1])
        parts = []
        for odd in range(2):
            rows = slice(odd * TILE, (odd + 1) * TILE)
            stacked = jnp.concatenate(
                [
                    jnp.concatenate([even_z[rows, :TILE], odd_z[rows, :TILE]], 1),
                    jnp.concatenate([even_z[rows, TILE:], odd_z[rows, TILE:]], 1),
                ],
                0,
            )
            parts.append(dot(fwd_left[odd], tall(stacked)))
        for side, values in enumerate((parts[0] + parts[1], parts[0] - parts[1])):
            values = values.reshape(2, 8, 2, 8, N)
            for part in range(2):
                field[2 * core, i, pl.ds(8 * side, 8), part] = values[part, :, 0]
                field[2 - core, i, pl.ds(8 * side, 8), part] = values[part, :, 1]

    def plane_and_pair(i, carry):
        plane_forward(i)
        pair(i).start()
        return carry

    for copy in early:
        copy.wait()
    plane_forward(0)
    pl.semaphore_wait(pltpu.get_barrier_semaphore(), len(peers))
    pair(0).start()
    for copy in spread:
        copy.start()
    lax.fori_loop(1, PLANES, plane_and_pair, 0)
    fetch_t.start()
    fetch_weights.start()
    for copy in late:
        copy.start()
    fetch.wait()
    for copy in spread:
        copy.wait_recv()
    bins_col[...] = bins_row[...].reshape(CHIPS * 8, SLOTS).T
    lane = lax.broadcasted_iota(jnp.int32, (SPAN, TILE), 1)

    def column(p, g):
        values = bins_col[pl.ds(g * SPAN, SPAN)]
        return jnp.sum(jnp.where(lane == 8 * p, values, 0.0), axis=1, keepdims=True).astype(jnp.int32)

    def slab_sums(g, px, py):
        p = py * RING + px
        index = column(p, g)
        kx, ky, side = index // 16, (index // 2) % 8, index % 2
        hot = jnp.where(lax.broadcasted_iota(jnp.int32, (SPAN, N), 1) == kx, 1.0, 0.0).astype(BF16)
        phase = dot(hot, table[...])
        row = lax.broadcasted_iota(jnp.int32, (SPAN, 4 * TILE), 1) % 8
        phase = jnp.where(row == ky, phase, 0.0).astype(BF16)
        mats = []
        for k in range(2):
            cosine, sine = phase[:, 2 * k * TILE : (2 * k + 1) * TILE], phase[:, (2 * k + 1) * TILE : (2 * k + 2) * TILE]
            mats.append(jnp.concatenate([jnp.concatenate([cosine, sine], 1), jnp.concatenate([-sine, cosine], 1)], 0))
        rows = jnp.concatenate([field[c, :, p, part].reshape(64, N) for part in range(2) for c in range(2)], 0)
        sums = dot(jnp.concatenate([mats[0], mats[1], mats[0]], 1), tall(rows))
        low_lane = jnp.where(lane < 64, 0, 1) == side
        sums_a[g, px, pl.ds(py * SPAN, SPAN)] = jnp.where(low_lane, sums[:SPAN, :TILE], sums[:SPAN, TILE:])
        sums_b[g, py, pl.ds(px * SPAN, SPAN)] = jnp.where(low_lane, sums[SPAN:, :TILE], sums[SPAN:, TILE:])

    def over_slabs(one):
        def far_column(k, carry):
            one(up(x, 2), up(y, k))
            return carry

        def far_row(k, carry):
            one(up(x, 3 + k), up(y, 2))
            return carry

        def near(k, carry):
            one(up(x, 3 + k % 3), up(y, 3 + k // 3))
            return carry

        return (
            lambda unroll: lax.fori_loop(0, 4, far_column, 0, unroll=unroll),
            lambda unroll: lax.fori_loop(0, 3, far_row, 0, unroll=unroll),
            lambda start, stop, unroll: lax.fori_loop(start, stop, near, 0, unroll=unroll),
        )

    first, second = [], []
    for g in range(GROUPS):
        for half in range(2):
            k = 2 * g + half
            ring = (x, east, west) if half == 0 else (y, north, south)
            src = (sums_a, sums_b)[half].at[g]
            first.append(RingSum(src, via_up1.at[k], via_down1.at[k], from_down1.at[k], from_up1.at[k], ring_send.at[k], ring_recv.at[k], *ring))
            me, others_k = (y, (device(x, up(y, 2), core), north, south)) if half == 0 else (x, (device(up(x, 2), y, core), east, west))
            second.append(RingDirect(mids.at[k], slots2.at[k], share_send.at[k], share_recv.at[k], me, others_k))
    gathers = []
    for g in range(GROUPS):
        gathers.append(
            (
                PlaneGather(all_a.at[g], all_send.at[2 * g], all_recv.at[2 * g], x, y, east, west, north, south),
                PlaneGather(all_b.at[g], all_send.at[2 * g + 1], all_recv.at[2 * g + 1], y, x, north, south, east, west),
            )
        )

    def rings(which, g, action):
        for ring in which[2 * g : 2 * g + 2]:
            getattr(ring, action)()

    def middle(g):
        for k in (2 * g, 2 * g + 1):
            first[k].arrive()
            for m in range(RING):
                mids[k, m] = first[k].total(pl.ds(m * SPAN, SPAN))
            second[k].begin()

    def own_upper(g):
        return jnp.concatenate([jnp.broadcast_to(column(chip, g) % 2, (SPAN, TILE)) == 1] * 4, 0)

    def grid_begin(g):
        rings(second, g, "arrive")
        values = jnp.concatenate([second[2 * g].total(), second[2 * g + 1].total()], 0)
        upper = own_upper(g)
        high = values.astype(BF16).astype(F32)
        both = jnp.concatenate([high, values - high], 0)
        both = jnp.concatenate([jnp.where(upper, 0.0, both), jnp.where(upper, both, 0.0)], 1).astype(BF16)
        mixed[...] = dot(both, natural[...]).reshape(4, SPAN, TILE)

    def grid_units(g, start, stop):
        def unit(k, carry):
            row = lax.broadcasted_iota(jnp.int32, (32, TILE), 0) % 8
            rows = [pl.ds(16 * k + 8 * u, 8) for u in range(2)]
            low = [mixed[:, r].reshape(32, TILE).astype(BF16) for r in rows]
            none = jnp.zeros((32, TILE), BF16)
            lhs = jnp.concatenate([jnp.concatenate([low[0], none], 1), jnp.concatenate([none, low[1]], 1)], 0)
            mat = jnp.concatenate([weight_buf[pl.ds(g * SPAN + 16 * k + 8 * u, 8)].reshape(8 * TILE, TILE) for u in range(2)], 1)
            spread = lax.dot_general(lhs, mat, (((1,), (1,)), ((), ())), preferred_element_type=F32)
            masked = []
            for u in range(2):
                samples = jnp.zeros((32, TILE), F32)
                for j in range(8):
                    samples = jnp.where(row == j, spread[32 * u : 32 * u + 32, j * TILE : (j + 1) * TILE], samples)
                samples = samples[:16] + samples[16:]
                high = samples.astype(BF16).astype(F32)
                both = jnp.concatenate([high, samples - high], 0)
                masked.append(jnp.concatenate([jnp.where(row == j, both, 0.0).astype(BF16) for j in range(8)], 1))
            back = dot(jnp.concatenate(masked, 0), mat)
            for u in range(2):
                values = back[32 * u : 32 * u + 32, u * TILE : (u + 1) * TILE]
                values = values[:16] + values[16:]
                gridded[0, rows[u]] = values[:8]
                gridded[1, rows[u]] = values[8:]
            return carry

        lax.fori_loop(start, stop, unit, 0, unroll=4)

    def grid_end(g):
        upper = own_upper(g)
        high, low = split(gridded[...].reshape(2 * SPAN, TILE))
        back = dot(jnp.concatenate([high, low], 0), packed[...])
        back = jnp.where(upper, back[:, TILE:], back[:, :TILE])
        back = back[: 2 * SPAN] + back[2 * SPAN :]
        slot = g * SPAN + lax.broadcasted_iota(jnp.int32, (2 * SPAN, TILE), 0) % SPAN
        back = jnp.where(slot < live[0], back, 0.0)
        all_a[g, x, y] = back[:SPAN]
        all_b[g, y, x] = back[SPAN:]

    def slab_pair(p):
        return remote(planes_back.at[2, p], planes_back.at[core, p], slab_send.at[p], slab_recv.at[p], sibling)

    def prepare(g):
        def one(p, carry):
            index = bins_row[p, 0:1, pl.ds(g * SPAN, SPAN)].astype(jnp.int32)
            kx, ky = index // 16, (index // 2) % 8
            hot = jnp.where(lax.broadcasted_iota(jnp.int32, (N, SPAN), 0) == kx, 1.0, 0.0).astype(BF16)
            phase = dot(table_t[...], hot)
            row = lax.broadcasted_iota(jnp.int32, (4 * TILE, SPAN), 0) % 8
            back_phase[g, p] = jnp.where(row == ky, phase, 0.0).astype(BF16)
            return carry

        return lambda start, stop: lax.fori_loop(start, stop, one, 0, unroll=2)

    def slab_back(g, px, py):
        p = py * RING + px
        side = column(p, g) % 2
        phase = back_phase[g, p]
        mats = []
        for k in range(2):
            cosine, sine = phase[2 * k * TILE : (2 * k + 1) * TILE], phase[(2 * k + 1) * TILE : (2 * k + 2) * TILE]
            mats.append(jnp.concatenate([jnp.concatenate([cosine, -sine], 1), jnp.concatenate([sine, cosine], 1)], 0))
        tiles = jnp.concatenate([all_a[g, px, py], all_b[g, py, px]], 0)
        low_lane = jnp.where(lane < 64, 0, 1) == side
        low_lane = jnp.concatenate([low_lane, low_lane], 0)
        tiles = jnp.concatenate([jnp.where(low_lane, tiles, 0.0), jnp.where(low_lane, 0.0, tiles)], 1)
        sums = dot(jnp.concatenate([mats[0], mats[1], mats[0]], 1), tall(tiles))
        sums = sums.reshape(2, 2, PLANES, 8, N)
        for part in range(2):
            for source, slot in ((0, 2 * core), (1, 2 - core)):
                values = sums[part, source]
                if g > 0:
                    values = values + planes_back[slot, p, :, part]
                planes_back[slot, p, :, part] = values
        if g == GROUPS - 1:
            slab_pair(p).start()

    def arrived(i, carry):
        pair(i).wait_recv()
        return carry

    def both(g, action, *args):
        for gather in gathers[g]:
            getattr(gather, action)(*args)

    sums = [over_slabs(functools.partial(slab_sums, g)) for g in range(GROUPS)]
    backs = [over_slabs(functools.partial(slab_back, g)) for g in range(GROUPS)]
    prepares = [prepare(g) for g in range(GROUPS)]

    def far_sums(g):
        sums[g][0](4)
        sums[g][1](3)

    def near_sums(g):
        sums[g][2](0, 4, 4)
        sums[g][2](5, 9, 4)

    lax.fori_loop(0, PLANES, arrived, 0)
    far_sums(0)
    rings(first, 0, "far")
    near_sums(0)
    rings(first, 0, "near")
    slab_sums(0, x, y)
    far_sums(1)
    rings(first, 0, "relay")
    rings(first, 1, "far")
    near_sums(1)
    slab_sums(1, x, y)
    fetch_t.wait()
    prepares[0](0, 16)
    middle(0)
    rings(first, 1, "near")
    prepares[1](0, 16)
    rings(first, 1, "relay")
    for copy in late:
        copy.wait()
    fetch_weights.wait()
    grid_begin(0)
    grid_units(0, 0, 8)
    middle(1)
    grid_end(0)
    both(0, "begin")
    both(0, "pass_inner")
    both(0, "relay", 0)
    grid_begin(1)
    grid_units(1, 0, 4)
    both(0, "last_inner")
    grid_units(1, 4, 8)
    grid_end(1)
    both(1, "begin")
    both(0, "relay", 1)
    both(0, "relay", 2)
    backs[0][2](0, 5, 5)
    both(0, "relay", 3)
    both(1, "pass_inner")
    backs[0][2](5, 9, 4)
    both(1, "relay", 0)
    both(1, "last_inner")
    for k in range(4):
        both(0, "last", k)
    backs[0][0](4)
    both(1, "relay", 1)
    both(1, "relay", 2)
    backs[0][1](3)
    backs[1][2](0, 5, 5)
    both(1, "relay", 3)
    backs[1][2](5, 9, 4)
    for k, step in enumerate((0, 3, 1, 2)):
        both(1, "last", k)
        slab_back(1, up(x, 2), up(y, step))
        if step != 2:
            slab_back(1, up(x, step), up(y, 2))

    def slabs_arrived(p, carry):
        slab_pair(p).wait_recv()
        return carry

    lax.fori_loop(0, CHIPS, slabs_arrived, 0)

    term = image_buf
    quarter = N // RING
    far, near_up, near_down = up(coil, 2), up(coil), down(coil)

    def share(part, i, q):
        return term.at[part, i, :, pl.ds(pl.multiple_of(q * quarter, quarter), quarter)]

    def coil_copy(i, k):
        source, target, peer = (
            (share(0, i, far), via_up.at[i], over),
            (share(1, i, far), via_down.at[i], under),
            (share(1, i, near_up), from_down.at[i, 1], over),
            (share(0, i, near_down), from_up.at[i, 0], under),
            (share(0, i, near_up), from_down.at[i, 0], over),
            (share(1, i, near_down), from_up.at[i, 1], under),
        )[k]
        return remote(source, target, coil_send.at[i, k], coil_recv.at[i, k], peer)

    def coil_relay(i):
        coil_copy(i, 0).wait_recv()
        ref = share(0, i, near_up)
        ref[...] = ref[...] + via_up[i]
        coil_copy(i, 4).start()
        coil_copy(i, 1).wait_recv()
        ref = share(1, i, near_down)
        ref[...] = ref[...] + via_down[i]
        coil_copy(i, 5).start()

    def plane_back(i, carry):
        near_half, far_half = planes_back[pl.ds(0, 2), pl.ds(0, 8), i], planes_back[pl.ds(0, 2), pl.ds(8, 8), i]
        even = dot(back_left[0], tall((near_half + far_half).reshape(N, N)))
        odd = dot(back_left[1], tall((near_half - far_half).reshape(N, N)))
        halves_z = []
        for k in range(2):
            lanes = slice(k * TILE, (k + 1) * TILE)
            stacked = jnp.concatenate([jnp.concatenate([v[:TILE, lanes], v[TILE:, lanes]], 1) for v in (even, odd)], 0)
            halves_z.append(dot(wide(stacked), back_right[k]))
        for half, values in enumerate((halves_z[0] + halves_z[1], halves_z[0] - halves_z[1])):
            for odd in range(2):
                rows = slice(odd * TILE, (odd + 1) * TILE)
                field_re, field_im = values[rows, :TILE], values[rows, TILE:]
                every = pl.ds(odd, TILE, stride=2)
                sens_re, sens_im = sens_buf[0, i, half, every, :], sens_buf[1, i, half, every, :]
                term[0, i, half, every, :] = sens_re * field_re + sens_im * field_im
                term[1, i, half, every, :] = sens_re * field_im - sens_im * field_re
        for k in range(4):
            coil_copy(i, k).start()
        return carry

    def plane_and_relay(i, carry):
        plane_back(i, carry)
        coil_relay(i - 2)
        return carry

    def sent(i, carry):
        pair(i).wait_send()
        slab_pair(2 * i).wait_send()
        slab_pair(2 * i + 1).wait_send()
        return carry

    lax.fori_loop(0, 2, plane_back, 0)
    for ring in first + second:
        ring.drain()
    for g in range(GROUPS):
        both(g, "drain")
    for copy in spread:
        copy.wait_send()
    lax.fori_loop(0, PLANES, sent, 0)
    lax.fori_loop(2, PLANES, plane_and_relay, 0)
    coil_relay(PLANES - 2)
    coil_relay(PLANES - 1)

    def store(i):
        return pltpu.make_async_copy(result.at[:, i], out.at[:, i], out_sem.at[i])

    def collect(i, carry):
        for k in (2, 3, 4, 5):
            coil_copy(i, k).wait_recv()
        for part in range(2):
            total = share(part, i, coil)[...] + from_down[i, part] + from_up[i, part]
            for half in range(2):
                result[part, i, :, half * TILE : (half + 1) * TILE] = total[half]
        store(i).start()
        for k in range(6):
            coil_copy(i, k).wait_send()
        return carry

    def finished(i, carry):
        store(i).wait()
        return carry

    lax.fori_loop(0, PLANES, collect, 0)
    lax.fori_loop(0, PLANES, finished, 0)


def fused(image, sens, bins, live, weights, tab):
    quarter = N // RING
    rings = 2 * GROUPS
    vmem = pl.BlockSpec(memory_space=pltpu.VMEM)
    hbm = pl.BlockSpec(memory_space=pl.ANY)
    smem = pl.BlockSpec(memory_space=pltpu.SMEM)
    return pl.pallas_call(
        kernel,
        out_shape=jax.ShapeDtypeStruct((2, PLANES, quarter, N), F32),
        in_specs=[hbm, hbm, vmem, smem] + [hbm] * 9,
        out_specs=hbm,
        scratch_shapes=[
            pltpu.VMEM((2, 3 * N, N), BF16),
            pltpu.VMEM((2, N, 3 * N), BF16),
            pltpu.VMEM((2, N, 3 * N), BF16),
            pltpu.VMEM((2, 3 * N, N), BF16),
            pltpu.VMEM((N, TILE), BF16),
            pltpu.VMEM((TILE, N), BF16),
            pltpu.VMEM((2, PLANES, 2, N, TILE), F32),
            pltpu.VMEM((2, PLANES, 2, N, TILE), F32),
            pltpu.VMEM((SLOTS, TILE, TILE), BF16),
            pltpu.VMEM((3, PLANES, CHIPS, 2, 8, N), F32),
            pltpu.VMEM((N, 4 * TILE), BF16),
            pltpu.VMEM((4 * TILE, N), BF16),
            pltpu.VMEM((CHIPS, 8, SLOTS), F32),
            pltpu.VMEM((SLOTS, CHIPS * 8), F32),
            pltpu.VMEM((GROUPS, RING, RING * SPAN, TILE), F32),
            pltpu.VMEM((GROUPS, RING, RING * SPAN, TILE), F32),
            pltpu.VMEM((rings, RING, SPAN, TILE), F32),
            pltpu.VMEM((rings, 2 * SPAN, TILE), F32),
            pltpu.VMEM((rings, 2 * SPAN, TILE), F32),
            pltpu.VMEM((rings, 4 * SPAN, TILE), F32),
            pltpu.VMEM((rings, 4 * SPAN, TILE), F32),
            pltpu.VMEM((rings, 3, SPAN, TILE), F32),
            pltpu.VMEM((4, SPAN, TILE), F32),
            pltpu.VMEM((2, SPAN, TILE), F32),
            pltpu.VMEM((GROUPS, CHIPS, 4 * TILE, SPAN), BF16),
            pltpu.VMEM((GROUPS, RING, RING, SPAN, TILE), F32),
            pltpu.VMEM((GROUPS, RING, RING, SPAN, TILE), F32),
            pltpu.VMEM((3, CHIPS, PLANES, 2, 8, N), F32),
            pltpu.VMEM((PLANES, 2, quarter, TILE), F32),
            pltpu.VMEM((PLANES, 2, quarter, TILE), F32),
            pltpu.VMEM((PLANES, 2, 2, quarter, TILE), F32),
            pltpu.VMEM((PLANES, 2, 2, quarter, TILE), F32),
            pltpu.VMEM((2, PLANES, quarter, N), F32),
            pltpu.SemaphoreType.DMA((PLANES, 4)),
            pltpu.SemaphoreType.DMA,
            pltpu.SemaphoreType.DMA((8,)),
            pltpu.SemaphoreType.DMA((PLANES,)),
            pltpu.SemaphoreType.DMA((CHIPS - 1,)),
            pltpu.SemaphoreType.DMA((CHIPS - 1,)),
            pltpu.SemaphoreType.DMA((PLANES,)),
            pltpu.SemaphoreType.DMA((PLANES,)),
            pltpu.SemaphoreType.DMA((rings, 6)),
            pltpu.SemaphoreType.DMA((rings, 6)),
            pltpu.SemaphoreType.DMA((rings, 3)),
            pltpu.SemaphoreType.DMA((rings, 3)),
            pltpu.SemaphoreType.DMA((rings, 20)),
            pltpu.SemaphoreType.DMA((rings, 20)),
            pltpu.SemaphoreType.DMA((CHIPS,)),
            pltpu.SemaphoreType.DMA((CHIPS,)),
            pltpu.SemaphoreType.DMA((PLANES, 6)),
            pltpu.SemaphoreType.DMA((PLANES, 6)),
        ],
        compiler_params=pltpu.CompilerParams(collective_id=0, has_side_effects=True, vmem_limit_bytes=VMEM_LIMIT),
    )(
        image, sens, bins, live, weights, tab["fwd_right"], tab["fwd_left"], tab["back_left"], tab["back_right"],
        tab["natural"], tab["packed"], tab["phases"], tab["phases_t"],
    )


def body(image, sens, weights, bins, counts):
    tab = {name: jnp.asarray(table) for name, table in tables().items()}
    return fused(image, sens, bins.reshape(1, SLOTS), counts, weights, tab)


def solution(mesh):
    in_specs = (
        P(None, "slab", None, None),
        P("coil", None, "slab", None, None),
        P("slab", None, None),
        P("slab"),
        P("slab"),
    )
    out_specs = P(None, "slab", "coil", None)
    return jax.shard_map(body, mesh=mesh, in_specs=in_specs, out_specs=out_specs, check_vma=False)
```

```python
import functools

import numpy as np
import jax
import jax.numpy as jnp
import ml_dtypes
from jax import lax
from jax.experimental import pallas as pl
from jax.experimental.pallas import tpu as pltpu
from jax.sharding import PartitionSpec as P

N = 256
TILE = 128
SLOTS = 256
CHIPS = 16
RING = 4
PLANES = 8
GROUPS = 2
SPAN = SLOTS // GROUPS
VMEM_LIMIT = 60 * 1024 * 1024
F32 = jnp.float32
BF16 = jnp.bfloat16


def halves(values):
    high = values.astype(ml_dtypes.bfloat16)
    low = (values - high.astype(np.float64)).astype(ml_dtypes.bfloat16)
    return high, low


def stack(table, axis):
    high, low = halves(table)
    return np.concatenate([high, low, high], axis)


def wave(rows, columns):
    angle = 2.0 * np.pi * (rows[:, None] * columns[None, :] % N) / N
    return np.cos(angle) / 16.0, np.sin(angle) / 16.0


EVEN = 2 * np.arange(TILE)
ODD = (2 * np.arange(TILE) + 1 + TILE) % N


def tables():
    first = np.arange(TILE)
    fwd_right, fwd_left, back_left, back_right = [], [], [], []
    packed = np.arange(2 * TILE).reshape(2, PLANES, 2, 8).transpose(2, 1, 0, 3).reshape(-1)
    for odd in range(2):
        cosine, sine = wave(first, (EVEN, ODD)[odd])
        fwd_right.append(stack(np.block([[cosine, -sine], [sine, cosine]]), 0))
        cosine, sine = wave((EVEN, ODD)[odd], first)
        back_right.append(stack(np.block([[cosine, sine], [-sine, cosine]]), 0))
        cosine, sine = wave(first, 2 * first + odd)
        fwd_left.append(stack(np.block([[cosine, sine], [-sine, cosine]]), 1))
        cosine, sine = wave(2 * first + odd, first)
        back_left.append(stack(np.block([[cosine, -sine], [sine, cosine]])[:, packed], 1))
    lanes = []
    cosine, sine = wave(np.arange(N), np.arange(N))
    for chip in range(CHIPS):
        cos_x = np.repeat(cosine[:, chip * 16 : chip * 16 + 16], 8, axis=1)
        sin_x = np.repeat(sine[:, chip * 16 : chip * 16 + 16], 8, axis=1)
        cos_parts, sin_parts = halves(cos_x), halves(sin_x)
        lanes.append(np.concatenate([cos_parts[0], sin_parts[0], cos_parts[1], sin_parts[1]], 1))
    phases = np.stack(lanes)
    lane = np.arange(TILE)
    order = np.stack([np.where(lane < 64, 2 * lane, 2 * lane - TILE + 1), np.where(lane < 64, 2 * lane + 1, 2 * lane - TILE)])
    natural = np.concatenate([np.eye(TILE)[order[0]], np.eye(TILE)[order[1]]], 0).astype(ml_dtypes.bfloat16)
    return {
        "fwd_right": np.stack(fwd_right),
        "fwd_left": np.stack(fwd_left),
        "back_left": np.stack(back_left),
        "back_right": np.stack(back_right),
        "phases": phases,
        "phases_t": np.ascontiguousarray(phases.transpose(0, 2, 1)),
        "natural": natural,
        "packed": np.ascontiguousarray(natural.T),
    }


def split(values):
    high = values.astype(BF16)
    low = (values - high.astype(F32)).astype(BF16)
    return high, low


def dot(a, b):
    return lax.dot_general(a, b, (((1,), (0,)), ((), ())), preferred_element_type=F32)


def wide(values):
    high, low = split(values)
    return jnp.concatenate([high, high, low], 1)


def tall(values):
    high, low = split(values)
    return jnp.concatenate([high, high, low], 0)


def place():
    slab = lax.axis_index("slab")
    core = lax.rem(slab, 2)
    chip = slab // 2
    x, y = lax.rem(chip, RING), chip // RING
    return core, chip, x, y


def device(x, y, core):
    return {"slab": (y * RING + x) * 2 + core}


def up(i, step=1):
    return lax.rem(i + step, RING)


def down(i):
    return lax.rem(i + RING - 1, RING)


def halved(source, target, sem, i, first):
    return [
        pltpu.make_async_copy(source.at[:, i, :, pl.ds(half * TILE, TILE)], target.at[:, i, half], sem.at[i, first])
        for half in range(2)
    ]


def greet(peers):
    barrier = pltpu.get_barrier_semaphore()
    for peer in peers:
        pl.semaphore_signal(barrier, inc=1, device_id=peer, device_id_type=pl.DeviceIdType.MESH)


def remote(src, dst, send, recv, peer):
    return pltpu.make_async_remote_copy(
        src_ref=src, dst_ref=dst, send_sem=send, recv_sem=recv, device_id=peer, device_id_type=pl.DeviceIdType.MESH
    )


def settle(ref, sem):
    pltpu.make_async_copy(ref, ref, sem).wait()


class RingSum:
    def __init__(self, src, via_up, via_down, from_down, from_up, send, recv, me, above, below):
        self.src, self.me = src, me
        rows = src.shape[1]
        self.half = (pl.ds(0, rows // 2), pl.ds(rows // 2, rows // 2))
        self.via_up, self.via_down, self.from_down, self.from_up = via_up, via_down, from_down, from_up
        first, second = self.half
        far, near_up, near_down = up(me, 2), up(me), down(me)
        self.send, self.recv = send, recv
        self.copies = [
            remote(src.at[far, first], via_up, send, recv.at[0], above),
            remote(src.at[far, second], via_down, send, recv.at[1], below),
            remote(src.at[near_up, second], from_down.at[second], send, recv.at[2], above),
            remote(src.at[near_down, first], from_up.at[first], send, recv.at[2], below),
            remote(src.at[near_up, first], from_down.at[first], send, recv.at[2], above),
            remote(src.at[near_down, second], from_up.at[second], send, recv.at[2], below),
        ]

    def far(self):
        for copy in self.copies[:2]:
            copy.start()

    def near(self):
        for copy in self.copies[2:4]:
            copy.start()

    def relay(self):
        first, second = self.half
        self.copies[0].wait_recv()
        near = up(self.me)
        self.src[near, first] = self.src[near, first] + self.via_up[...]
        self.copies[4].start()
        self.copies[1].wait_recv()
        near = down(self.me)
        self.src[near, second] = self.src[near, second] + self.via_down[...]
        self.copies[5].start()

    def arrive(self):
        settle(self.src.at[pl.ds(0, 2)], self.recv.at[2])

    def total(self, rows):
        return self.src[self.me, rows] + self.from_down[rows] + self.from_up[rows]

    def drain(self):
        settle(self.src.at[pl.ds(0, 3)], self.send)


class RingDirect:
    def __init__(self, src, slots, send, recv, me, peers):
        self.src, self.slots, self.me, self.send, self.recv = src, slots, me, send, recv
        self.copies = [
            remote(src.at[up(me, step)], slots.at[k], send, recv, peer)
            for k, (step, peer) in enumerate(zip((2, 1, 3), peers))
        ]

    def begin(self):
        for copy in self.copies:
            copy.start()

    def arrive(self):
        settle(self.slots, self.recv)

    def total(self):
        return self.src[self.me] + self.slots[0] + self.slots[1] + self.slots[2]

    def drain(self):
        settle(self.slots, self.send)


class PlaneGather:
    def __init__(self, buf, send, recv, outer, inner, outer_up, outer_down, inner_up, inner_down):
        rows = buf.shape[2]
        first, second = pl.ds(0, rows // 2), pl.ds(rows // 2, rows // 2)
        row, below, above = buf.at[outer], buf.at[down(outer)], buf.at[up(outer)]

        self.buf, self.send, self.recv = buf, send, recv

        def same(ref, s, r, peer):
            return remote(ref, ref, send.at[s], recv.at[r], peer)

        self.inner = [
            same(row.at[inner], 0, 0, inner_up),
            same(row.at[inner], 0, 0, inner_down),
            same(row.at[down(inner), first], 0, 1, inner_up),
            same(row.at[up(inner), second], 0, 1, inner_down),
        ]
        pieces = [inner, down(inner), up(inner), up(inner, 2)]
        self.direct = [(same(row.at[p], 1, 2 + k, outer_up), same(row.at[p], 1, 2 + k, outer_down)) for k, p in enumerate(pieces)]
        self.relays = [
            (same(below.at[p, first], 1, 6 + k, outer_up), same(above.at[p, second], 1, 6 + k, outer_down))
            for k, p in enumerate(pieces)
        ]

    def some(self, pieces):
        return self.buf.at[0, pl.ds(0, pieces)]

    def begin(self):
        for copy in self.inner[:2] + list(self.direct[0]):
            copy.start()

    def pass_inner(self):
        settle(self.some(2), self.recv.at[0])
        for copy in self.inner[2:] + list(self.direct[1] + self.direct[2]):
            copy.start()

    def last_inner(self):
        settle(self.some(1), self.recv.at[1])
        for copy in self.direct[3]:
            copy.start()

    def relay(self, piece):
        settle(self.some(2), self.recv.at[2 + piece])
        for copy in self.relays[piece]:
            copy.start()

    def last(self, piece):
        settle(self.some(1), self.recv.at[6 + piece])

    def drain(self):
        settle(self.some(3), self.send.at[0])
        settle(self.buf.at[pl.ds(0, 3)], self.send.at[1])


def kernel(
    image, sens, bins, live, weights, fwd_right_hbm, fwd_left_hbm, back_left_hbm, back_right_hbm, natural_hbm, packed_hbm, phases, phases_t, out,
    fwd_right, fwd_left, back_left, back_right, natural, packed, image_buf, sens_buf, weight_buf, field, table, table_t, bins_row, bins_col, sums_a, sums_b, mids,
    via_up1, via_down1, from_down1, from_up1, slots2,
    mixed, gridded, back_phase, all_a, all_b, planes_back, via_up, via_down, from_down, from_up, result,
    load_sem, weight_sem, table_sem, out_sem, bin_send, bin_recv, pair_send, pair_recv, ring_send, ring_recv, share_send, share_recv,
    all_send, all_recv, slab_send, slab_recv, coil_send, coil_recv,
):
    core, chip, x, y = place()
    coil = lax.axis_index("coil")
    sibling = device(x, y, 1 - core)
    east, west = device(up(x), y, core), device(down(x), y, core)
    north, south = device(x, up(y), core), device(x, down(y), core)
    over, under = {"coil": up(coil)}, {"coil": down(coil)}
    others = [{"slab": lax.rem(chip + k, CHIPS) * 2 + core} for k in range(1, CHIPS)]
    peers = [sibling, over, under] + others
    def loads(i):
        return halved(image, image_buf, load_sem, i, 0) + halved(sens.at[0], sens_buf, load_sem, i, 1)

    def start_load(i, carry):
        for copy in loads(i):
            copy.start()
        return carry

    early = [pltpu.make_async_copy(fwd_right_hbm, fwd_right, table_sem.at[2]), pltpu.make_async_copy(fwd_left_hbm, fwd_left, table_sem.at[3])]
    late = [
        pltpu.make_async_copy(source, target, table_sem.at[4 + k])
        for k, (source, target) in enumerate(
            ((back_left_hbm, back_left), (back_right_hbm, back_right), (natural_hbm, natural), (packed_hbm, packed))
        )
    ]
    fetch = pltpu.make_async_copy(phases.at[chip], table, table_sem.at[0])
    fetch_t = pltpu.make_async_copy(phases_t.at[chip], table_t, table_sem.at[1])
    fetch_weights = pltpu.make_async_copy(weights, weight_buf, weight_sem)
    start_load(0, 0)
    for copy in early:
        copy.start()
    greet(peers)
    lax.fori_loop(1, PLANES, start_load, 0)
    fetch.start()
    bins_row[chip] = jnp.broadcast_to(bins[...].astype(F32), (8, SLOTS))
    spread = [remote(bins_row.at[chip], bins_row.at[chip], bin_send, bin_recv, others[k]) for k in range(CHIPS - 1)]

    def pair(i):
        return remote(field.at[2, i], field.at[core, i], pair_send, pair_recv, sibling)

    def plane_forward(i):
        settle(image_buf.at[:, i], load_sem.at[i, 0])
        settle(sens_buf.at[:, i], load_sem.at[i, 1])
        summed, differed = [], []
        for odd in range(2):
            rows = pl.ds(odd, TILE, stride=2)
            parts = []
            for half in range(2):
                image_re, image_im = image_buf[0, i, half, rows, :], image_buf[1, i, half, rows, :]
                sens_re, sens_im = sens_buf[0, i, half, rows, :], sens_buf[1, i, half, rows, :]
                parts.append((sens_re * image_re - sens_im * image_im, sens_re * image_im + sens_im * image_re))
            summed.append(jnp.concatenate([parts[0][k] + parts[1][k] for k in range(2)], 1))
            differed.append(jnp.concatenate([parts[0][k] - parts[1][k] for k in range(2)], 1))
        even_z = dot(wide(jnp.concatenate(summed, 0)), fwd_right[0])
        odd_z = dot(wide(jnp.concatenate(differed, 0)), fwd_right[1])
        parts = []
        for odd in range(2):
            rows = slice(odd * TILE, (odd + 1) * TILE)
            stacked = jnp.concatenate(
                [
                    jnp.concatenate([even_z[rows, :TILE], odd_z[rows, :TILE]], 1),
                    jnp.concatenate([even_z[rows, TILE:], odd_z[rows, TILE:]], 1),
                ],
                0,
            )
            parts.append(dot(fwd_left[odd], tall(stacked)))
        for side, values in enumerate((parts[0] + parts[1], parts[0] - parts[1])):
            values = values.reshape(2, 8, 2, 8, N)
            for part in range(2):
                field[2 * core, i, pl.ds(8 * side, 8), part] = values[part, :, 0]
                field[2 - core, i, pl.ds(8 * side, 8), part] = values[part, :, 1]

    def plane_and_pair(i, carry):
        plane_forward(i)
        pair(i).start()
        return carry

    for copy in early:
        copy.wait()
    plane_forward(0)
    pl.semaphore_wait(pltpu.get_barrier_semaphore(), len(peers))
    pair(0).start()
    for copy in spread:
        copy.start()
    lax.fori_loop(1, PLANES, plane_and_pair, 0)
    fetch_t.start()
    fetch_weights.start()
    for copy in late:
        copy.start()
    fetch.wait()
    settle(bins_row.at[pl.ds(0, CHIPS - 1)], bin_recv)
    bins_col[...] = bins_row[...].reshape(CHIPS * 8, SLOTS).T
    lane = lax.broadcasted_iota(jnp.int32, (SPAN, TILE), 1)

    def column(p, g):
        values = bins_col[pl.ds(g * SPAN, SPAN)]
        return jnp.sum(jnp.where(lane == 8 * p, values, 0.0), axis=1, keepdims=True).astype(jnp.int32)

    def slab_sums(g, px, py):
        p = py * RING + px
        index = column(p, g)
        kx, ky, side = index // 16, (index // 2) % 8, index % 2
        hot = jnp.where(lax.broadcasted_iota(jnp.int32, (SPAN, N), 1) == kx, 1.0, 0.0).astype(BF16)
        phase = dot(hot, table[...])
        row = lax.broadcasted_iota(jnp.int32, (SPAN, 4 * TILE), 1) % 8
        phase = jnp.where(row == ky, phase, 0.0).astype(BF16)
        mats = []
        for k in range(2):
            cosine, sine = phase[:, 2 * k * TILE : (2 * k + 1) * TILE], phase[:, (2 * k + 1) * TILE : (2 * k + 2) * TILE]
            mats.append(jnp.concatenate([jnp.concatenate([cosine, sine], 1), jnp.concatenate([-sine, cosine], 1)], 0))
        rows = jnp.concatenate([field[c, :, p, part].reshape(64, N) for part in range(2) for c in range(2)], 0)
        sums = dot(jnp.concatenate([mats[0], mats[1], mats[0]], 1), tall(rows))
        low_lane = jnp.where(lane < 64, 0, 1) == side
        sums_a[g, px, pl.ds(py * SPAN, SPAN)] = jnp.where(low_lane, sums[:SPAN, :TILE], sums[:SPAN, TILE:])
        sums_b[g, py, pl.ds(px * SPAN, SPAN)] = jnp.where(low_lane, sums[SPAN:, :TILE], sums[SPAN:, TILE:])

    def over_slabs(one):
        def far_column(k, carry):
            one(up(x, 2), up(y, k))
            return carry

        def far_row(k, carry):
            one(up(x, 3 + k), up(y, 2))
            return carry

        def near(k, carry):
            one(up(x, 3 + k % 3), up(y, 3 + k // 3))
            return carry

        return (
            lambda unroll: lax.fori_loop(0, 4, far_column, 0, unroll=unroll),
            lambda unroll: lax.fori_loop(0, 3, far_row, 0, unroll=unroll),
            lambda start, stop, unroll: lax.fori_loop(start, stop, near, 0, unroll=unroll),
        )

    first, second = [], []
    for g in range(GROUPS):
        for half in range(2):
            k = 2 * g + half
            ring = (x, east, west) if half == 0 else (y, north, south)
            src = (sums_a, sums_b)[half].at[g]
            first.append(RingSum(src, via_up1.at[k], via_down1.at[k], from_down1.at[k], from_up1.at[k], ring_send.at[k], ring_recv.at[k], *ring))
            me, others_k = (y, (device(x, up(y, 2), core), north, south)) if half == 0 else (x, (device(up(x, 2), y, core), east, west))
            second.append(RingDirect(mids.at[k], slots2.at[k], share_send.at[k], share_recv.at[k], me, others_k))
    gathers = []
    for g in range(GROUPS):
        gathers.append(
            (
                PlaneGather(all_a.at[g], all_send.at[2 * g], all_recv.at[2 * g], x, y, east, west, north, south),
                PlaneGather(all_b.at[g], all_send.at[2 * g + 1], all_recv.at[2 * g + 1], y, x, north, south, east, west),
            )
        )

    def rings(which, g, action):
        for ring in which[2 * g : 2 * g + 2]:
            getattr(ring, action)()

    def middle(g):
        for k in (2 * g, 2 * g + 1):
            first[k].arrive()
            for m in range(RING):
                mids[k, m] = first[k].total(pl.ds(m * SPAN, SPAN))
            second[k].begin()

    def own_upper(g):
        return jnp.concatenate([jnp.broadcast_to(column(chip, g) % 2, (SPAN, TILE)) == 1] * 4, 0)

    def grid_begin(g):
        rings(second, g, "arrive")
        values = jnp.concatenate([second[2 * g].total(), second[2 * g + 1].total()], 0)
        upper = own_upper(g)
        high = values.astype(BF16).astype(F32)
        both = jnp.concatenate([high, values - high], 0)
        both = jnp.concatenate([jnp.where(upper, 0.0, both), jnp.where(upper, both, 0.0)], 1).astype(BF16)
        mixed[...] = dot(both, natural[...]).reshape(4, SPAN, TILE)

    def grid_units(g, start, stop):
        def unit(k, carry):
            row = lax.broadcasted_iota(jnp.int32, (32, TILE), 0) % 8
            rows = [pl.ds(16 * k + 8 * u, 8) for u in range(2)]
            low = [mixed[:, r].reshape(32, TILE).astype(BF16) for r in rows]
            none = jnp.zeros((32, TILE), BF16)
            lhs = jnp.concatenate([jnp.concatenate([low[0], none], 1), jnp.concatenate([none, low[1]], 1)], 0)
            mat = jnp.concatenate([weight_buf[pl.ds(g * SPAN + 16 * k + 8 * u, 8)].reshape(8 * TILE, TILE) for u in range(2)], 1)
            spread = lax.dot_general(lhs, mat, (((1,), (1,)), ((), ())), preferred_element_type=F32)
            masked = []
            for u in range(2):
                samples = jnp.zeros((32, TILE), F32)
                for j in range(8):
                    samples = jnp.where(row == j, spread[32 * u : 32 * u + 32, j * TILE : (j + 1) * TILE], samples)
                samples = samples[:16] + samples[16:]
                high = samples.astype(BF16).astype(F32)
                both = jnp.concatenate([high, samples - high], 0)
                masked.append(jnp.concatenate([jnp.where(row == j, both, 0.0).astype(BF16) for j in range(8)], 1))
            back = dot(jnp.concatenate(masked, 0), mat)
            for u in range(2):
                values = back[32 * u : 32 * u + 32, u * TILE : (u + 1) * TILE]
                values = values[:16] + values[16:]
                gridded[0, rows[u]] = values[:8]
                gridded[1, rows[u]] = values[8:]
            return carry

        lax.fori_loop(start, stop, unit, 0, unroll=4)

    def grid_end(g):
        upper = own_upper(g)
        high, low = split(gridded[...].reshape(2 * SPAN, TILE))
        back = dot(jnp.concatenate([high, low], 0), packed[...])
        back = jnp.where(upper, back[:, TILE:], back[:, :TILE])
        back = back[: 2 * SPAN] + back[2 * SPAN :]
        slot = g * SPAN + lax.broadcasted_iota(jnp.int32, (2 * SPAN, TILE), 0) % SPAN
        back = jnp.where(slot < live[0], back, 0.0)
        all_a[g, x, y] = back[:SPAN]
        all_b[g, y, x] = back[SPAN:]

    def slab_pair(p):
        return remote(planes_back.at[2, p], planes_back.at[core, p], slab_send, slab_recv, sibling)

    def prepare(g):
        def one(p, carry):
            index = bins_row[p, 0:1, pl.ds(g * SPAN, SPAN)].astype(jnp.int32)
            kx, ky = index // 16, (index // 2) % 8
            hot = jnp.where(lax.broadcasted_iota(jnp.int32, (N, SPAN), 0) == kx, 1.0, 0.0).astype(BF16)
            phase = dot(table_t[...], hot)
            row = lax.broadcasted_iota(jnp.int32, (4 * TILE, SPAN), 0) % 8
            back_phase[g, p] = jnp.where(row == ky, phase, 0.0).astype(BF16)
            return carry

        return lambda start, stop: lax.fori_loop(start, stop, one, 0, unroll=2)

    def slab_back(g, px, py):
        p = py * RING + px
        side = column(p, g) % 2
        phase = back_phase[g, p]
        mats = []
        for k in range(2):
            cosine, sine = phase[2 * k * TILE : (2 * k + 1) * TILE], phase[(2 * k + 1) * TILE : (2 * k + 2) * TILE]
            mats.append(jnp.concatenate([jnp.concatenate([cosine, -sine], 1), jnp.concatenate([sine, cosine], 1)], 0))
        tiles = jnp.concatenate([all_a[g, px, py], all_b[g, py, px]], 0)
        low_lane = jnp.where(lane < 64, 0, 1) == side
        low_lane = jnp.concatenate([low_lane, low_lane], 0)
        tiles = jnp.concatenate([jnp.where(low_lane, tiles, 0.0), jnp.where(low_lane, 0.0, tiles)], 1)
        sums = dot(jnp.concatenate([mats[0], mats[1], mats[0]], 1), tall(tiles))
        sums = sums.reshape(2, 2, PLANES, 8, N)
        for part in range(2):
            for source, slot in ((0, 2 * core), (1, 2 - core)):
                values = sums[part, source]
                if g > 0:
                    values = values + planes_back[slot, p, :, part]
                planes_back[slot, p, :, part] = values
        if g == GROUPS - 1:
            slab_pair(p).start()

    def both(g, action, *args):
        for gather in gathers[g]:
            getattr(gather, action)(*args)

    sums = [over_slabs(functools.partial(slab_sums, g)) for g in range(GROUPS)]
    backs = [over_slabs(functools.partial(slab_back, g)) for g in range(GROUPS)]
    prepares = [prepare(g) for g in range(GROUPS)]

    def far_sums(g):
        sums[g][0](4)
        sums[g][1](3)

    def near_sums(g):
        sums[g][2](0, 4, 4)
        sums[g][2](5, 9, 4)

    settle(field.at[2], pair_recv)
    far_sums(0)
    rings(first, 0, "far")
    near_sums(0)
    rings(first, 0, "near")
    slab_sums(0, x, y)
    far_sums(1)
    rings(first, 0, "relay")
    rings(first, 1, "far")
    near_sums(1)
    slab_sums(1, x, y)
    fetch_t.wait()
    prepares[0](0, 16)
    middle(0)
    rings(first, 1, "near")
    prepares[1](0, 16)
    rings(first, 1, "relay")
    for copy in late:
        copy.wait()
    fetch_weights.wait()
    grid_begin(0)
    grid_units(0, 0, 8)
    middle(1)
    grid_end(0)
    both(0, "begin")
    both(0, "pass_inner")
    both(0, "relay", 0)
    grid_begin(1)
    grid_units(1, 0, 4)
    both(0, "last_inner")
    grid_units(1, 4, 8)
    grid_end(1)
    both(1, "begin")
    both(0, "relay", 1)
    both(0, "relay", 2)
    backs[0][2](0, 5, 5)
    both(0, "relay", 3)
    both(1, "pass_inner")
    backs[0][2](5, 9, 4)
    both(1, "relay", 0)
    both(1, "last_inner")
    for k in range(4):
        both(0, "last", k)
    backs[0][0](4)
    both(1, "relay", 1)
    both(1, "relay", 2)
    backs[0][1](3)
    backs[1][2](0, 5, 5)
    both(1, "relay", 3)
    backs[1][2](5, 9, 4)
    for k, step in enumerate((0, 3, 1, 2)):
        both(1, "last", k)
        slab_back(1, up(x, 2), up(y, step))
        if step != 2:
            slab_back(1, up(x, step), up(y, 2))

    settle(planes_back.at[2], slab_recv)

    term = image_buf
    quarter = N // RING
    far, near_up, near_down = up(coil, 2), up(coil), down(coil)

    def share(part, i, q):
        return term.at[part, i, :, pl.ds(pl.multiple_of(q * quarter, quarter), quarter)]

    def coil_copy(i, k):
        source, target, peer = (
            (share(0, i, far), via_up.at[i], over),
            (share(1, i, far), via_down.at[i], under),
            (share(1, i, near_up), from_down.at[i, 1], over),
            (share(0, i, near_down), from_up.at[i, 0], under),
            (share(0, i, near_up), from_down.at[i, 0], over),
            (share(1, i, near_down), from_up.at[i, 1], under),
        )[k]
        return remote(source, target, coil_send.at[k // 4], coil_recv.at[i, min(k, 2)], peer)

    def coil_relay(i):
        coil_copy(i, 0).wait_recv()
        ref = share(0, i, near_up)
        ref[...] = ref[...] + via_up[i]
        coil_copy(i, 4).start()
        coil_copy(i, 1).wait_recv()
        ref = share(1, i, near_down)
        ref[...] = ref[...] + via_down[i]
        coil_copy(i, 5).start()

    def plane_back(i, carry):
        near_half, far_half = planes_back[pl.ds(0, 2), pl.ds(0, 8), i], planes_back[pl.ds(0, 2), pl.ds(8, 8), i]
        even = dot(back_left[0], tall((near_half + far_half).reshape(N, N)))
        odd = dot(back_left[1], tall((near_half - far_half).reshape(N, N)))
        halves_z = []
        for k in range(2):
            lanes = slice(k * TILE, (k + 1) * TILE)
            stacked = jnp.concatenate([jnp.concatenate([v[:TILE, lanes], v[TILE:, lanes]], 1) for v in (even, odd)], 0)
            halves_z.append(dot(wide(stacked), back_right[k]))
        for half, values in enumerate((halves_z[0] + halves_z[1], halves_z[0] - halves_z[1])):
            for odd in range(2):
                rows = slice(odd * TILE, (odd + 1) * TILE)
                field_re, field_im = values[rows, :TILE], values[rows, TILE:]
                every = pl.ds(odd, TILE, stride=2)
                sens_re, sens_im = sens_buf[0, i, half, every, :], sens_buf[1, i, half, every, :]
                term[0, i, half, every, :] = sens_re * field_re + sens_im * field_im
                term[1, i, half, every, :] = sens_re * field_im - sens_im * field_re
        for k in range(4):
            coil_copy(i, k).start()
        return carry

    def plane_and_relay(i, carry):
        plane_back(i, carry)
        coil_relay(i - 2)
        return carry

    lax.fori_loop(0, 2, plane_back, 0)
    for ring in first + second:
        ring.drain()
    for g in range(GROUPS):
        both(g, "drain")
    settle(bins_row.at[pl.ds(0, CHIPS - 1)], bin_send)
    settle(field.at[2], pair_send)
    settle(planes_back.at[2], slab_send)
    lax.fori_loop(2, PLANES, plane_and_relay, 0)
    coil_relay(PLANES - 2)
    coil_relay(PLANES - 1)

    def store(i):
        return pltpu.make_async_copy(result.at[:, i], out.at[:, i], out_sem)

    def collect(i, carry):
        settle(from_down.at[pl.ds(0, 2)], coil_recv.at[i, 2])
        for part in range(2):
            total = share(part, i, coil)[...] + from_down[i, part] + from_up[i, part]
            for half in range(2):
                result[part, i, :, half * TILE : (half + 1) * TILE] = total[half]
        store(i).start()
        return carry

    lax.fori_loop(0, PLANES, collect, 0)
    settle(field.at[2], coil_send.at[0])
    settle(from_down, coil_send.at[1])
    settle(result, out_sem)


def fused(image, sens, bins, live, weights, tab):
    quarter = N // RING
    rings = 2 * GROUPS
    vmem = pl.BlockSpec(memory_space=pltpu.VMEM)
    hbm = pl.BlockSpec(memory_space=pl.ANY)
    smem = pl.BlockSpec(memory_space=pltpu.SMEM)
    return pl.pallas_call(
        kernel,
        out_shape=jax.ShapeDtypeStruct((2, PLANES, quarter, N), F32),
        in_specs=[hbm, hbm, vmem, smem] + [hbm] * 9,
        out_specs=hbm,
        scratch_shapes=[
            pltpu.VMEM((2, 3 * N, N), BF16),
            pltpu.VMEM((2, N, 3 * N), BF16),
            pltpu.VMEM((2, N, 3 * N), BF16),
            pltpu.VMEM((2, 3 * N, N), BF16),
            pltpu.VMEM((N, TILE), BF16),
            pltpu.VMEM((TILE, N), BF16),
            pltpu.VMEM((2, PLANES, 2, N, TILE), F32),
            pltpu.VMEM((2, PLANES, 2, N, TILE), F32),
            pltpu.VMEM((SLOTS, TILE, TILE), BF16),
            pltpu.VMEM((3, PLANES, CHIPS, 2, 8, N), F32),
            pltpu.VMEM((N, 4 * TILE), BF16),
            pltpu.VMEM((4 * TILE, N), BF16),
            pltpu.VMEM((CHIPS, 8, SLOTS), F32),
            pltpu.VMEM((SLOTS, CHIPS * 8), F32),
            pltpu.VMEM((GROUPS, RING, RING * SPAN, TILE), F32),
            pltpu.VMEM((GROUPS, RING, RING * SPAN, TILE), F32),
            pltpu.VMEM((rings, RING, SPAN, TILE), F32),
            pltpu.VMEM((rings, 2 * SPAN, TILE), F32),
            pltpu.VMEM((rings, 2 * SPAN, TILE), F32),
            pltpu.VMEM((rings, 4 * SPAN, TILE), F32),
            pltpu.VMEM((rings, 4 * SPAN, TILE), F32),
            pltpu.VMEM((rings, 3, SPAN, TILE), F32),
            pltpu.VMEM((4, SPAN, TILE), F32),
            pltpu.VMEM((2, SPAN, TILE), F32),
            pltpu.VMEM((GROUPS, CHIPS, 4 * TILE, SPAN), BF16),
            pltpu.VMEM((GROUPS, RING, RING, SPAN, TILE), F32),
            pltpu.VMEM((GROUPS, RING, RING, SPAN, TILE), F32),
            pltpu.VMEM((3, CHIPS, PLANES, 2, 8, N), F32),
            pltpu.VMEM((PLANES, 2, quarter, TILE), F32),
            pltpu.VMEM((PLANES, 2, quarter, TILE), F32),
            pltpu.VMEM((PLANES, 2, 2, quarter, TILE), F32),
            pltpu.VMEM((PLANES, 2, 2, quarter, TILE), F32),
            pltpu.VMEM((2, PLANES, quarter, N), F32),
            pltpu.SemaphoreType.DMA((PLANES, 2)),
            pltpu.SemaphoreType.DMA,
            pltpu.SemaphoreType.DMA((8,)),
            pltpu.SemaphoreType.DMA,
            pltpu.SemaphoreType.DMA,
            pltpu.SemaphoreType.DMA,
            pltpu.SemaphoreType.DMA,
            pltpu.SemaphoreType.DMA,
            pltpu.SemaphoreType.DMA((rings,)),
            pltpu.SemaphoreType.DMA((rings, 3)),
            pltpu.SemaphoreType.DMA((rings,)),
            pltpu.SemaphoreType.DMA((rings,)),
            pltpu.SemaphoreType.DMA((rings, 2)),
            pltpu.SemaphoreType.DMA((rings, 10)),
            pltpu.SemaphoreType.DMA,
            pltpu.SemaphoreType.DMA,
            pltpu.SemaphoreType.DMA((2,)),
            pltpu.SemaphoreType.DMA((PLANES, 3)),
        ],
        compiler_params=pltpu.CompilerParams(collective_id=0, has_side_effects=True, vmem_limit_bytes=VMEM_LIMIT),
    )(
        image, sens, bins, live, weights, tab["fwd_right"], tab["fwd_left"], tab["back_left"], tab["back_right"],
        tab["natural"], tab["packed"], tab["phases"], tab["phases_t"],
    )


def body(image, sens, weights, bins, counts):
    tab = {name: jnp.asarray(table) for name, table in tables().items()}
    return fused(image, sens, bins.reshape(1, SLOTS), counts, weights, tab)


def solution(mesh):
    in_specs = (
        P(None, "slab", None, None),
        P("coil", None, "slab", None, None),
        P("slab", None, None),
        P("slab"),
        P("slab"),
    )
    out_specs = P(None, "slab", "coil", None)
    return jax.shard_map(body, mesh=mesh, in_specs=in_specs, out_specs=out_specs, check_vma=False)
```

```python
import functools

import numpy as np
import jax
import jax.numpy as jnp
import ml_dtypes
from jax import lax
from jax.experimental import pallas as pl
from jax.experimental.pallas import tpu as pltpu
from jax.sharding import PartitionSpec as P

N = 256
TILE = 128
SLOTS = 256
CHIPS = 16
RING = 4
PLANES = 8
GROUPS = 2
SPAN = SLOTS // GROUPS
VMEM_LIMIT = 60 * 1024 * 1024
F32 = jnp.float32
BF16 = jnp.bfloat16


def halves(values):
    high = values.astype(ml_dtypes.bfloat16)
    low = (values - high.astype(np.float64)).astype(ml_dtypes.bfloat16)
    return high, low


def stack(table, axis):
    high, low = halves(table)
    return np.concatenate([high, low, high], axis)


def wave(rows, columns):
    angle = 2.0 * np.pi * (rows[:, None] * columns[None, :] % N) / N
    return np.cos(angle) / 16.0, np.sin(angle) / 16.0


EVEN = 2 * np.arange(TILE)
ODD = (2 * np.arange(TILE) + 1 + TILE) % N


def tables():
    first = np.arange(TILE)
    fwd_right, fwd_left, back_left, back_right = [], [], [], []
    packed = np.arange(2 * TILE).reshape(2, PLANES, 2, 8).transpose(2, 1, 0, 3).reshape(-1)
    for odd in range(2):
        cosine, sine = wave(first, (EVEN, ODD)[odd])
        fwd_right.append(stack(np.block([[cosine, -sine], [sine, cosine]]), 0))
        cosine, sine = wave((EVEN, ODD)[odd], first)
        back_right.append(stack(np.block([[cosine, sine], [-sine, cosine]]), 0))
        cosine, sine = wave(first, 2 * first + odd)
        fwd_left.append(stack(np.block([[cosine, sine], [-sine, cosine]]), 1))
        cosine, sine = wave(2 * first + odd, first)
        back_left.append(stack(np.block([[cosine, -sine], [sine, cosine]])[:, packed], 1))
    lanes = []
    cosine, sine = wave(np.arange(N), np.arange(N))
    for chip in range(CHIPS):
        cos_x = np.repeat(cosine[:, chip * 16 : chip * 16 + 16], 8, axis=1)
        sin_x = np.repeat(sine[:, chip * 16 : chip * 16 + 16], 8, axis=1)
        cos_parts, sin_parts = halves(cos_x), halves(sin_x)
        lanes.append(np.concatenate([cos_parts[0], sin_parts[0], cos_parts[1], sin_parts[1]], 1))
    phases = np.stack(lanes)
    lane = np.arange(TILE)
    order = np.stack([np.where(lane < 64, 2 * lane, 2 * lane - TILE + 1), np.where(lane < 64, 2 * lane + 1, 2 * lane - TILE)])
    natural = np.concatenate([np.eye(TILE)[order[0]], np.eye(TILE)[order[1]]], 0).astype(ml_dtypes.bfloat16)
    return {
        "fwd_right": np.stack(fwd_right),
        "fwd_left": np.stack(fwd_left),
        "back_left": np.stack(back_left),
        "back_right": np.stack(back_right),
        "phases": phases,
        "phases_t": np.ascontiguousarray(phases.transpose(0, 2, 1)),
        "natural": natural,
        "packed": np.ascontiguousarray(natural.T),
    }


def split(values):
    high = values.astype(BF16)
    low = (values - high.astype(F32)).astype(BF16)
    return high, low


def dot(a, b):
    return lax.dot_general(a, b, (((1,), (0,)), ((), ())), preferred_element_type=F32)


def wide(values):
    high, low = split(values)
    return jnp.concatenate([high, high, low], 1)


def tall(values):
    high, low = split(values)
    return jnp.concatenate([high, high, low], 0)


def place():
    slab = lax.axis_index("slab")
    core = lax.rem(slab, 2)
    chip = slab // 2
    x, y = lax.rem(chip, RING), chip // RING
    return core, chip, x, y


def device(x, y, core):
    return {"slab": (y * RING + x) * 2 + core}


def up(i, step=1):
    return lax.rem(i + step, RING)


def down(i):
    return lax.rem(i + RING - 1, RING)


def halved(source, target, sem, i, first):
    return [
        pltpu.make_async_copy(source.at[:, i, :, pl.ds(half * TILE, TILE)], target.at[:, i, half], sem.at[i, first])
        for half in range(2)
    ]


def greet(peers):
    barrier = pltpu.get_barrier_semaphore()
    for peer in peers:
        pl.semaphore_signal(barrier, inc=1, device_id=peer, device_id_type=pl.DeviceIdType.MESH)


def remote(src, dst, send, recv, peer):
    return pltpu.make_async_remote_copy(
        src_ref=src, dst_ref=dst, send_sem=send, recv_sem=recv, device_id=peer, device_id_type=pl.DeviceIdType.MESH
    )


def settle(ref, sem):
    pltpu.make_async_copy(ref, ref, sem).wait()


class RingSum:
    def __init__(self, src, via_up, via_down, from_down, from_up, send, recv, me, above, below):
        self.src, self.me = src, me
        rows = src.shape[1]
        self.half = (pl.ds(0, rows // 2), pl.ds(rows // 2, rows // 2))
        self.via_up, self.via_down, self.from_down, self.from_up = via_up, via_down, from_down, from_up
        first, second = self.half
        far, near_up, near_down = up(me, 2), up(me), down(me)
        self.send, self.recv = send, recv
        self.copies = [
            remote(src.at[far, first], via_up, send, recv.at[0], above),
            remote(src.at[far, second], via_down, send, recv.at[0], below),
            remote(src.at[near_up, second], from_down.at[second], send, recv.at[1], above),
            remote(src.at[near_down, first], from_up.at[first], send, recv.at[1], below),
            remote(src.at[near_up, first], from_down.at[first], send, recv.at[1], above),
            remote(src.at[near_down, second], from_up.at[second], send, recv.at[1], below),
        ]

    def far(self):
        for copy in self.copies[:2]:
            copy.start()

    def near(self):
        for copy in self.copies[2:4]:
            copy.start()

    def relay(self):
        first, second = self.half
        settle(self.src.at[0], self.recv.at[0])
        near = up(self.me)
        self.src[near, first] = self.src[near, first] + self.via_up[...]
        self.copies[4].start()
        near = down(self.me)
        self.src[near, second] = self.src[near, second] + self.via_down[...]
        self.copies[5].start()

    def arrive(self):
        settle(self.src.at[pl.ds(0, 2)], self.recv.at[1])

    def total(self, rows):
        return self.src[self.me, rows] + self.from_down[rows] + self.from_up[rows]

    def drain(self):
        settle(self.src.at[pl.ds(0, 3)], self.send)


class RingDirect:
    def __init__(self, src, slots, send, recv, me, peers):
        self.src, self.slots, self.me, self.send, self.recv = src, slots, me, send, recv
        self.copies = [
            remote(src.at[up(me, step)], slots.at[k], send, recv, peer)
            for k, (step, peer) in enumerate(zip((2, 1, 3), peers))
        ]

    def begin(self):
        for copy in self.copies:
            copy.start()

    def arrive(self):
        settle(self.slots, self.recv)

    def total(self):
        return self.src[self.me] + self.slots[0] + self.slots[1] + self.slots[2]

    def drain(self):
        settle(self.slots, self.send)


class PlaneGather:
    def __init__(self, buf, send, recv, outer, inner, outer_up, outer_down, inner_up, inner_down):
        rows = buf.shape[2]
        first, second = pl.ds(0, rows // 2), pl.ds(rows // 2, rows // 2)
        row, below, above = buf.at[outer], buf.at[down(outer)], buf.at[up(outer)]

        self.buf, self.send, self.recv = buf, send, recv

        def same(ref, s, r, peer):
            return remote(ref, ref, send.at[s], recv.at[r], peer)

        self.inner = [
            same(row.at[inner], 0, 0, inner_up),
            same(row.at[inner], 0, 0, inner_down),
            same(row.at[down(inner), first], 0, 1, inner_up),
            same(row.at[up(inner), second], 0, 1, inner_down),
        ]
        pieces = [inner, down(inner), up(inner), up(inner, 2)]
        self.direct = [(same(row.at[p], 1, 2 + k, outer_up), same(row.at[p], 1, 2 + k, outer_down)) for k, p in enumerate(pieces)]
        self.relays = [
            (same(below.at[p, first], 1, 6 + k, outer_up), same(above.at[p, second], 1, 6 + k, outer_down))
            for k, p in enumerate(pieces)
        ]

    def some(self, pieces):
        return self.buf.at[0, pl.ds(0, pieces)]

    def begin(self):
        for copy in self.inner[:2] + list(self.direct[0]):
            copy.start()

    def pass_inner(self):
        settle(self.some(2), self.recv.at[0])
        for copy in self.inner[2:] + list(self.direct[1] + self.direct[2]):
            copy.start()

    def last_inner(self):
        settle(self.some(1), self.recv.at[1])
        for copy in self.direct[3]:
            copy.start()

    def relay(self, piece):
        settle(self.some(2), self.recv.at[2 + piece])
        for copy in self.relays[piece]:
            copy.start()

    def last(self, piece):
        settle(self.some(1), self.recv.at[6 + piece])

    def drain(self):
        settle(self.some(3), self.send.at[0])
        settle(self.buf.at[pl.ds(0, 3)], self.send.at[1])


def kernel(
    image, sens, bins, live, weights, fwd_right_hbm, fwd_left_hbm, back_left_hbm, back_right_hbm, natural_hbm, packed_hbm, phases, phases_t, out,
    fwd_right, fwd_left, back_left, back_right, natural, packed, image_buf, sens_buf, weight_buf, field, table, table_t, bins_row, bins_col, sums_a, sums_b, mids,
    via_up1, via_down1, from_down1, from_up1, slots2,
    mixed, gridded, back_phase, all_a, all_b, planes_back, via_up, via_down, from_down, from_up, result,
    load_sem, weight_sem, table_sem, out_sem, bin_send, bin_recv, pair_send, pair_recv, ring_send, ring_recv, share_send, share_recv,
    all_send, all_recv, slab_send, slab_recv, coil_send, coil_recv,
):
    core, chip, x, y = place()
    coil = lax.axis_index("coil")
    sibling = device(x, y, 1 - core)
    east, west = device(up(x), y, core), device(down(x), y, core)
    north, south = device(x, up(y), core), device(x, down(y), core)
    over, under = {"coil": up(coil)}, {"coil": down(coil)}
    others = [{"slab": lax.rem(chip + k, CHIPS) * 2 + core} for k in range(1, CHIPS)]
    peers = [sibling, over, under] + others
    def loads(i):
        return halved(image, image_buf, load_sem, i, 0) + halved(sens.at[0], sens_buf, load_sem, i, 1)

    def start_load(i, carry):
        for copy in loads(i):
            copy.start()
        return carry

    early = [pltpu.make_async_copy(fwd_right_hbm, fwd_right, table_sem.at[2]), pltpu.make_async_copy(fwd_left_hbm, fwd_left, table_sem.at[3])]
    late = [
        pltpu.make_async_copy(source, target, table_sem.at[4 + k])
        for k, (source, target) in enumerate(
            ((back_left_hbm, back_left), (back_right_hbm, back_right), (natural_hbm, natural), (packed_hbm, packed))
        )
    ]
    fetch = pltpu.make_async_copy(phases.at[chip], table, table_sem.at[0])
    fetch_t = pltpu.make_async_copy(phases_t.at[chip], table_t, table_sem.at[1])
    fetch_weights = pltpu.make_async_copy(weights, weight_buf, weight_sem)
    start_load(0, 0)
    for copy in early:
        copy.start()
    greet(peers)
    lax.fori_loop(1, PLANES, start_load, 0)
    fetch.start()
    bins_row[chip] = jnp.broadcast_to(bins[...].astype(F32), (8, SLOTS))
    spread = [remote(bins_row.at[chip], bins_row.at[chip], bin_send, bin_recv, others[k]) for k in range(CHIPS - 1)]

    def pair(i):
        return remote(field.at[2, i], field.at[core, i], pair_send, pair_recv, sibling)

    def plane_forward(i):
        settle(image_buf.at[:, i], load_sem.at[i, 0])
        settle(sens_buf.at[:, i], load_sem.at[i, 1])
        summed, differed = [], []
        for odd in range(2):
            rows = pl.ds(odd, TILE, stride=2)
            parts = []
            for half in range(2):
                image_re, image_im = image_buf[0, i, half, rows, :], image_buf[1, i, half, rows, :]
                sens_re, sens_im = sens_buf[0, i, half, rows, :], sens_buf[1, i, half, rows, :]
                parts.append((sens_re * image_re - sens_im * image_im, sens_re * image_im + sens_im * image_re))
            summed.append(jnp.concatenate([parts[0][k] + parts[1][k] for k in range(2)], 1))
            differed.append(jnp.concatenate([parts[0][k] - parts[1][k] for k in range(2)], 1))
        even_z = dot(wide(jnp.concatenate(summed, 0)), fwd_right[0])
        odd_z = dot(wide(jnp.concatenate(differed, 0)), fwd_right[1])
        parts = []
        for odd in range(2):
            rows = slice(odd * TILE, (odd + 1) * TILE)
            stacked = jnp.concatenate(
                [
                    jnp.concatenate([even_z[rows, :TILE], odd_z[rows, :TILE]], 1),
                    jnp.concatenate([even_z[rows, TILE:], odd_z[rows, TILE:]], 1),
                ],
                0,
            )
            parts.append(dot(fwd_left[odd], tall(stacked)))
        for side, values in enumerate((parts[0] + parts[1], parts[0] - parts[1])):
            values = values.reshape(2, 8, 2, 8, N)
            for part in range(2):
                field[2 * core, i, pl.ds(8 * side, 8), part] = values[part, :, 0]
                field[2 - core, i, pl.ds(8 * side, 8), part] = values[part, :, 1]

    def plane_and_pair(i, carry):
        plane_forward(i)
        pair(i).start()
        return carry

    for copy in early:
        copy.wait()
    plane_forward(0)
    pl.semaphore_wait(pltpu.get_barrier_semaphore(), len(peers))
    pair(0).start()
    for copy in spread:
        copy.start()
    lax.fori_loop(1, PLANES, plane_and_pair, 0)
    fetch_t.start()
    fetch_weights.start()
    for copy in late:
        copy.start()
    fetch.wait()
    settle(bins_row.at[pl.ds(0, CHIPS - 1)], bin_recv)
    bins_col[...] = bins_row[...].reshape(CHIPS * 8, SLOTS).T
    lane = lax.broadcasted_iota(jnp.int32, (SPAN, TILE), 1)

    def column(p, g):
        values = bins_col[pl.ds(g * SPAN, SPAN)]
        return jnp.sum(jnp.where(lane == 8 * p, values, 0.0), axis=1, keepdims=True).astype(jnp.int32)

    def slab_sums(g, px, py):
        p = py * RING + px
        index = column(p, g)
        kx, ky, side = index // 16, (index // 2) % 8, index % 2
        hot = jnp.where(lax.broadcasted_iota(jnp.int32, (SPAN, N), 1) == kx, 1.0, 0.0).astype(BF16)
        phase = dot(hot, table[...])
        row = lax.broadcasted_iota(jnp.int32, (SPAN, 4 * TILE), 1) % 8
        phase = jnp.where(row == ky, phase, 0.0).astype(BF16)
        mats = []
        for k in range(2):
            cosine, sine = phase[:, 2 * k * TILE : (2 * k + 1) * TILE], phase[:, (2 * k + 1) * TILE : (2 * k + 2) * TILE]
            mats.append(jnp.concatenate([jnp.concatenate([cosine, sine], 1), jnp.concatenate([-sine, cosine], 1)], 0))
        rows = jnp.concatenate([field[c, :, p, part].reshape(64, N) for part in range(2) for c in range(2)], 0)
        sums = dot(jnp.concatenate([mats[0], mats[1], mats[0]], 1), tall(rows))
        low_lane = jnp.where(lane < 64, 0, 1) == side
        sums_a[g, px, pl.ds(py * SPAN, SPAN)] = jnp.where(low_lane, sums[:SPAN, :TILE], sums[:SPAN, TILE:])
        sums_b[g, py, pl.ds(px * SPAN, SPAN)] = jnp.where(low_lane, sums[SPAN:, :TILE], sums[SPAN:, TILE:])

    def over_slabs(one):
        def far_column(k, carry):
            one(up(x, 2), up(y, k))
            return carry

        def far_row(k, carry):
            one(up(x, 3 + k), up(y, 2))
            return carry

        def near(k, carry):
            one(up(x, 3 + k % 3), up(y, 3 + k // 3))
            return carry

        return (
            lambda unroll: lax.fori_loop(0, 4, far_column, 0, unroll=unroll),
            lambda unroll: lax.fori_loop(0, 3, far_row, 0, unroll=unroll),
            lambda start, stop, unroll: lax.fori_loop(start, stop, near, 0, unroll=unroll),
        )

    first, second = [], []
    for g in range(GROUPS):
        for half in range(2):
            k = 2 * g + half
            ring = (x, east, west) if half == 0 else (y, north, south)
            src = (sums_a, sums_b)[half].at[g]
            first.append(RingSum(src, via_up1.at[k], via_down1.at[k], from_down1.at[k], from_up1.at[k], ring_send.at[k], ring_recv.at[k], *ring))
            me, others_k = (y, (device(x, up(y, 2), core), north, south)) if half == 0 else (x, (device(up(x, 2), y, core), east, west))
            second.append(RingDirect(mids.at[k], slots2.at[k], share_send.at[k], share_recv.at[k], me, others_k))
    gathers = []
    for g in range(GROUPS):
        gathers.append(
            (
                PlaneGather(all_a.at[g], all_send.at[2 * g], all_recv.at[2 * g], x, y, east, west, north, south),
                PlaneGather(all_b.at[g], all_send.at[2 * g + 1], all_recv.at[2 * g + 1], y, x, north, south, east, west),
            )
        )

    def rings(which, g, action):
        for ring in which[2 * g : 2 * g + 2]:
            getattr(ring, action)()

    def middle(g):
        for k in (2 * g, 2 * g + 1):
            first[k].arrive()
            for m in range(RING):
                mids[k, m] = first[k].total(pl.ds(m * SPAN, SPAN))
            second[k].begin()

    def own_upper(g):
        return jnp.concatenate([jnp.broadcast_to(column(chip, g) % 2, (SPAN, TILE)) == 1] * 4, 0)

    def grid_begin(g):
        rings(second, g, "arrive")
        values = jnp.concatenate([second[2 * g].total(), second[2 * g + 1].total()], 0)
        upper = own_upper(g)
        high = values.astype(BF16).astype(F32)
        both = jnp.concatenate([high, values - high], 0)
        both = jnp.concatenate([jnp.where(upper, 0.0, both), jnp.where(upper, both, 0.0)], 1).astype(BF16)
        mixed[...] = dot(both, natural[...]).reshape(4, SPAN, TILE)

    def grid_units(g, start, stop):
        def unit(k, carry):
            row = lax.broadcasted_iota(jnp.int32, (32, TILE), 0) % 8
            rows = [pl.ds(16 * k + 8 * u, 8) for u in range(2)]
            low = [mixed[:, r].reshape(32, TILE).astype(BF16) for r in rows]
            none = jnp.zeros((32, TILE), BF16)
            lhs = jnp.concatenate([jnp.concatenate([low[0], none], 1), jnp.concatenate([none, low[1]], 1)], 0)
            mat = jnp.concatenate([weight_buf[pl.ds(g * SPAN + 16 * k + 8 * u, 8)].reshape(8 * TILE, TILE) for u in range(2)], 1)
            spread = lax.dot_general(lhs, mat, (((1,), (1,)), ((), ())), preferred_element_type=F32)
            masked = []
            for u in range(2):
                samples = jnp.zeros((32, TILE), F32)
                for j in range(8):
                    samples = jnp.where(row == j, spread[32 * u : 32 * u + 32, j * TILE : (j + 1) * TILE], samples)
                samples = samples[:16] + samples[16:]
                high = samples.astype(BF16).astype(F32)
                both = jnp.concatenate([high, samples - high], 0)
                masked.append(jnp.concatenate([jnp.where(row == j, both, 0.0).astype(BF16) for j in range(8)], 1))
            back = dot(jnp.concatenate(masked, 0), mat)
            for u in range(2):
                values = back[32 * u : 32 * u + 32, u * TILE : (u + 1) * TILE]
                values = values[:16] + values[16:]
                gridded[0, rows[u]] = values[:8]
                gridded[1, rows[u]] = values[8:]
            return carry

        lax.fori_loop(start, stop, unit, 0, unroll=4)

    def grid_end(g):
        upper = own_upper(g)
        high, low = split(gridded[...].reshape(2 * SPAN, TILE))
        back = dot(jnp.concatenate([high, low], 0), packed[...])
        back = jnp.where(upper, back[:, TILE:], back[:, :TILE])
        back = back[: 2 * SPAN] + back[2 * SPAN :]
        slot = g * SPAN + lax.broadcasted_iota(jnp.int32, (2 * SPAN, TILE), 0) % SPAN
        back = jnp.where(slot < live[0], back, 0.0)
        all_a[g, x, y] = back[:SPAN]
        all_b[g, y, x] = back[SPAN:]

    def slab_pair(p):
        return remote(planes_back.at[2, p], planes_back.at[core, p], slab_send, slab_recv, sibling)

    def prepare(g):
        def one(p, carry):
            index = bins_row[p, 0:1, pl.ds(g * SPAN, SPAN)].astype(jnp.int32)
            kx, ky = index // 16, (index // 2) % 8
            hot = jnp.where(lax.broadcasted_iota(jnp.int32, (N, SPAN), 0) == kx, 1.0, 0.0).astype(BF16)
            phase = dot(table_t[...], hot)
            row = lax.broadcasted_iota(jnp.int32, (4 * TILE, SPAN), 0) % 8
            back_phase[g, p] = jnp.where(row == ky, phase, 0.0).astype(BF16)
            return carry

        return lambda start, stop: lax.fori_loop(start, stop, one, 0, unroll=2)

    def slab_back(g, px, py):
        p = py * RING + px
        side = column(p, g) % 2
        phase = back_phase[g, p]
        mats = []
        for k in range(2):
            cosine, sine = phase[2 * k * TILE : (2 * k + 1) * TILE], phase[(2 * k + 1) * TILE : (2 * k + 2) * TILE]
            mats.append(jnp.concatenate([jnp.concatenate([cosine, -sine], 1), jnp.concatenate([sine, cosine], 1)], 0))
        tiles = jnp.concatenate([all_a[g, px, py], all_b[g, py, px]], 0)
        low_lane = jnp.where(lane < 64, 0, 1) == side
        low_lane = jnp.concatenate([low_lane, low_lane], 0)
        tiles = jnp.concatenate([jnp.where(low_lane, tiles, 0.0), jnp.where(low_lane, 0.0, tiles)], 1)
        sums = dot(jnp.concatenate([mats[0], mats[1], mats[0]], 1), tall(tiles))
        sums = sums.reshape(2, 2, PLANES, 8, N)
        for part in range(2):
            for source, slot in ((0, 2 * core), (1, 2 - core)):
                values = sums[part, source]
                if g > 0:
                    values = values + planes_back[slot, p, :, part]
                planes_back[slot, p, :, part] = values
        if g == GROUPS - 1:
            slab_pair(p).start()

    def both(g, action, *args):
        for gather in gathers[g]:
            getattr(gather, action)(*args)

    sums = [over_slabs(functools.partial(slab_sums, g)) for g in range(GROUPS)]
    backs = [over_slabs(functools.partial(slab_back, g)) for g in range(GROUPS)]
    prepares = [prepare(g) for g in range(GROUPS)]

    def far_sums(g):
        sums[g][0](4)
        if g == 0:
            first[0].far()
        sums[g][1](3)

    def near_sums(g):
        sums[g][2](0, 4, 4)
        sums[g][2](5, 9, 4)

    settle(field.at[2], pair_recv)
    far_sums(0)
    first[1].far()
    near_sums(0)
    rings(first, 0, "near")
    slab_sums(0, x, y)
    far_sums(1)
    rings(first, 0, "relay")
    rings(first, 1, "far")
    near_sums(1)
    slab_sums(1, x, y)
    fetch_t.wait()
    prepares[0](0, 16)
    middle(0)
    rings(first, 1, "near")
    prepares[1](0, 16)
    rings(first, 1, "relay")
    for copy in late:
        copy.wait()
    fetch_weights.wait()
    grid_begin(0)
    grid_units(0, 0, 8)
    middle(1)
    grid_end(0)
    both(0, "begin")
    both(0, "pass_inner")
    both(0, "relay", 0)
    grid_begin(1)
    grid_units(1, 0, 4)
    both(0, "last_inner")
    grid_units(1, 4, 8)
    grid_end(1)
    both(1, "begin")
    both(0, "relay", 1)
    both(0, "relay", 2)
    backs[0][2](0, 5, 5)
    both(0, "relay", 3)
    both(1, "pass_inner")
    backs[0][2](5, 9, 4)
    both(1, "relay", 0)
    both(1, "last_inner")
    for k in range(4):
        both(0, "last", k)
    backs[0][0](4)
    both(1, "relay", 1)
    both(1, "relay", 2)
    backs[0][1](3)
    backs[1][2](0, 5, 5)
    both(1, "relay", 3)
    backs[1][2](5, 9, 4)
    for k, step in enumerate((0, 3, 1, 2)):
        both(1, "last", k)
        slab_back(1, up(x, 2), up(y, step))
        if step != 2:
            slab_back(1, up(x, step), up(y, 2))

    settle(planes_back.at[2], slab_recv)

    term = image_buf
    quarter = N // RING
    far, near_up, near_down = up(coil, 2), up(coil), down(coil)

    def share(part, i, q):
        return term.at[part, i, :, pl.ds(pl.multiple_of(q * quarter, quarter), quarter)]

    def coil_copy(i, k):
        source, target, peer = (
            (share(0, i, far), via_up.at[i], over),
            (share(1, i, far), via_down.at[i], under),
            (share(1, i, near_up), from_down.at[i, 1], over),
            (share(0, i, near_down), from_up.at[i, 0], under),
            (share(0, i, near_up), from_down.at[i, 0], over),
            (share(1, i, near_down), from_up.at[i, 1], under),
        )[k]
        return remote(source, target, coil_send.at[k // 4], coil_recv.at[i, min(k // 2, 1)], peer)

    def coil_relay(i):
        settle(from_down.at[0], coil_recv.at[i, 0])
        ref = share(0, i, near_up)
        ref[...] = ref[...] + via_up[i]
        coil_copy(i, 4).start()
        ref = share(1, i, near_down)
        ref[...] = ref[...] + via_down[i]
        coil_copy(i, 5).start()

    def plane_back(i, carry):
        near_half, far_half = planes_back[pl.ds(0, 2), pl.ds(0, 8), i], planes_back[pl.ds(0, 2), pl.ds(8, 8), i]
        even = dot(back_left[0], tall((near_half + far_half).reshape(N, N)))
        odd = dot(back_left[1], tall((near_half - far_half).reshape(N, N)))
        halves_z = []
        for k in range(2):
            lanes = slice(k * TILE, (k + 1) * TILE)
            stacked = jnp.concatenate([jnp.concatenate([v[:TILE, lanes], v[TILE:, lanes]], 1) for v in (even, odd)], 0)
            halves_z.append(dot(wide(stacked), back_right[k]))
        for half, values in enumerate((halves_z[0] + halves_z[1], halves_z[0] - halves_z[1])):
            for odd in range(2):
                rows = slice(odd * TILE, (odd + 1) * TILE)
                field_re, field_im = values[rows, :TILE], values[rows, TILE:]
                every = pl.ds(odd, TILE, stride=2)
                sens_re, sens_im = sens_buf[0, i, half, every, :], sens_buf[1, i, half, every, :]
                term[0, i, half, every, :] = sens_re * field_re + sens_im * field_im
                term[1, i, half, every, :] = sens_re * field_im - sens_im * field_re
        for k in range(4):
            coil_copy(i, k).start()
        return carry

    def plane_and_relay(i, carry):
        plane_back(i, carry)
        coil_relay(i - 2)
        return carry

    lax.fori_loop(0, 2, plane_back, 0)
    for ring in first + second:
        ring.drain()
    for g in range(GROUPS):
        both(g, "drain")
    settle(bins_row.at[pl.ds(0, CHIPS - 1)], bin_send)
    settle(field.at[2], pair_send)
    settle(planes_back.at[2], slab_send)
    lax.fori_loop(2, PLANES, plane_and_relay, 0)
    coil_relay(PLANES - 2)
    coil_relay(PLANES - 1)

    def store(i):
        return pltpu.make_async_copy(result.at[:, i], out.at[:, i], out_sem)

    def collect(i, carry):
        settle(from_down.at[pl.ds(0, 2)], coil_recv.at[i, 1])
        for part in range(2):
            total = share(part, i, coil)[...] + from_down[i, part] + from_up[i, part]
            for half in range(2):
                result[part, i, :, half * TILE : (half + 1) * TILE] = total[half]
        store(i).start()
        return carry

    lax.fori_loop(0, PLANES, collect, 0)
    settle(field.at[2], coil_send.at[0])
    settle(from_down, coil_send.at[1])
    settle(result, out_sem)


def fused(image, sens, bins, live, weights, tab):
    quarter = N // RING
    rings = 2 * GROUPS
    vmem = pl.BlockSpec(memory_space=pltpu.VMEM)
    hbm = pl.BlockSpec(memory_space=pl.ANY)
    smem = pl.BlockSpec(memory_space=pltpu.SMEM)
    return pl.pallas_call(
        kernel,
        out_shape=jax.ShapeDtypeStruct((2, PLANES, quarter, N), F32),
        in_specs=[hbm, hbm, vmem, smem] + [hbm] * 9,
        out_specs=hbm,
        scratch_shapes=[
            pltpu.VMEM((2, 3 * N, N), BF16),
            pltpu.VMEM((2, N, 3 * N), BF16),
            pltpu.VMEM((2, N, 3 * N), BF16),
            pltpu.VMEM((2, 3 * N, N), BF16),
            pltpu.VMEM((N, TILE), BF16),
            pltpu.VMEM((TILE, N), BF16),
            pltpu.VMEM((2, PLANES, 2, N, TILE), F32),
            pltpu.VMEM((2, PLANES, 2, N, TILE), F32),
            pltpu.VMEM((SLOTS, TILE, TILE), BF16),
            pltpu.VMEM((3, PLANES, CHIPS, 2, 8, N), F32),
            pltpu.VMEM((N, 4 * TILE), BF16),
            pltpu.VMEM((4 * TILE, N), BF16),
            pltpu.VMEM((CHIPS, 8, SLOTS), F32),
            pltpu.VMEM((SLOTS, CHIPS * 8), F32),
            pltpu.VMEM((GROUPS, RING, RING * SPAN, TILE), F32),
            pltpu.VMEM((GROUPS, RING, RING * SPAN, TILE), F32),
            pltpu.VMEM((rings, RING, SPAN, TILE), F32),
            pltpu.VMEM((rings, 2 * SPAN, TILE), F32),
            pltpu.VMEM((rings, 2 * SPAN, TILE), F32),
            pltpu.VMEM((rings, 4 * SPAN, TILE), F32),
            pltpu.VMEM((rings, 4 * SPAN, TILE), F32),
            pltpu.VMEM((rings, 3, SPAN, TILE), F32),
            pltpu.VMEM((4, SPAN, TILE), F32),
            pltpu.VMEM((2, SPAN, TILE), F32),
            pltpu.VMEM((GROUPS, CHIPS, 4 * TILE, SPAN), BF16),
            pltpu.VMEM((GROUPS, RING, RING, SPAN, TILE), F32),
            pltpu.VMEM((GROUPS, RING, RING, SPAN, TILE), F32),
            pltpu.VMEM((3, CHIPS, PLANES, 2, 8, N), F32),
            pltpu.VMEM((PLANES, 2, quarter, TILE), F32),
            pltpu.VMEM((PLANES, 2, quarter, TILE), F32),
            pltpu.VMEM((PLANES, 2, 2, quarter, TILE), F32),
            pltpu.VMEM((PLANES, 2, 2, quarter, TILE), F32),
            pltpu.VMEM((2, PLANES, quarter, N), F32),
            pltpu.SemaphoreType.DMA((PLANES, 2)),
            pltpu.SemaphoreType.DMA,
            pltpu.SemaphoreType.DMA((8,)),
            pltpu.SemaphoreType.DMA,
            pltpu.SemaphoreType.DMA,
            pltpu.SemaphoreType.DMA,
            pltpu.SemaphoreType.DMA,
            pltpu.SemaphoreType.DMA,
            pltpu.SemaphoreType.DMA((rings,)),
            pltpu.SemaphoreType.DMA((rings, 2)),
            pltpu.SemaphoreType.DMA((rings,)),
            pltpu.SemaphoreType.DMA((rings,)),
            pltpu.SemaphoreType.DMA((rings, 2)),
            pltpu.SemaphoreType.DMA((rings, 10)),
            pltpu.SemaphoreType.DMA,
            pltpu.SemaphoreType.DMA,
            pltpu.SemaphoreType.DMA((2,)),
            pltpu.SemaphoreType.DMA((PLANES, 2)),
        ],
        compiler_params=pltpu.CompilerParams(collective_id=0, has_side_effects=True, vmem_limit_bytes=VMEM_LIMIT),
    )(
        image, sens, bins, live, weights, tab["fwd_right"], tab["fwd_left"], tab["back_left"], tab["back_right"],
        tab["natural"], tab["packed"], tab["phases"], tab["phases_t"],
    )


def body(image, sens, weights, bins, counts):
    tab = {name: jnp.asarray(table) for name, table in tables().items()}
    return fused(image, sens, bins.reshape(1, SLOTS), counts, weights, tab)


def solution(mesh):
    in_specs = (
        P(None, "slab", None, None),
        P("coil", None, "slab", None, None),
        P("slab", None, None),
        P("slab"),
        P("slab"),
    )
    out_specs = P(None, "slab", "coil", None)
    return jax.shard_map(body, mesh=mesh, in_specs=in_specs, out_specs=out_specs, check_vma=False)
```
